256 devices in a mesh: sample: 8 (over x_hi, y), space: 32 (over x_lo, z, core).
Axes of the slice: x: 4 (x_hi: 2, x_lo: 2; x = x_hi * 2 + x_lo), y: 4, z: 8, core: 2. Of those that a mesh axis runs over, the one named last changes fastest.
Arguments:
- activations: bfloat16 [8, 64, 8, 1024], P('sample', 'space'), may hold values from -100 to 100
- cotangent: bfloat16 [8, 64, 8, 2048], P('sample', 'space'), may hold values from -100 to 100
- weight: bfloat16 [128, 1728], replicated, may hold values from -0.15625 to 0.15625
- a_inverse: float32 [1728, 1728], P('space'), may hold values from -0.2 to 4.2, as said below
- g_inverse: float32 [128, 128], replicated, may hold values from -0.2 to 4.2, as said below
Outputs:
- outputs: bfloat16 [8, 64, 8, 2048], P('sample', 'space')
- input_grad: bfloat16 [8, 64, 8, 1024], P('sample', 'space')
- a_factor: float32 [1728, 1728], P('space')
- g_factor: float32 [128, 128], replicated
- update: float32 [128, 1728], P(None, 'space')
The draws below stay inside these ranges and needn't reach their ends.
Inputs may be any that keep to these rules, and one draw needn't show every extreme that they name: `a_inverse`: symmetric. `g_inverse`: symmetric.
All inputs are finite; a program needn't handle non-finite values.
Results may differ from the reference program's by a relative error of at most 0.013.
Values may be sent and summed in bfloat16 or wider, within the bound.
A program may use at most 64 MiB of HBM per device.

```python
import math
import jax
import jax.numpy as jnp
from jax import lax

CIN = 64
COUT = 128
NY = 8
NZ = 16
KC = 1728
SAMPLES = 8
NX = 64


def shared_field(key):
    normal = jax.random.normal(key, (SAMPLES, NX, NY, NZ, CIN), jnp.float32)
    return normal


def position_scale():
    index = jnp.arange(NX, dtype=jnp.float32)
    return jnp.exp(math.log(3.0) * index / max(NX - 1, 1)).reshape(1, NX, 1, 1, 1)


def symmetric_matrix(key, size, lowest, highest):
    key_diag, key_off = jax.random.split(key)
    diagonal = jnp.exp(jax.random.uniform(key_diag, (size,), jnp.float32, math.log(lowest), math.log(highest)))
    bound = 0.7 / math.sqrt(size)
    offdiag = jax.random.uniform(key_off, (size, size), jnp.float32, -bound, bound)
    return 0.5 * (offdiag + offdiag.T) + jnp.diag(diagonal)


def draw_activations(key, part):
    base = shared_field(key)
    mixed = base + 0.4 * jnp.roll(base, 1, axis=4) + 0.3 * jnp.roll(base, 1, axis=3)
    return (mixed * position_scale()).reshape(SAMPLES, NX, NY, NZ * CIN).astype(jnp.bfloat16)


def draw_cotangent(key, part):
    base = shared_field(key)
    key = jax.random.fold_in(key, 5)
    noise = jax.random.normal(key, (SAMPLES, NX, NY, NZ, COUT), jnp.float32)
    paired = jnp.concatenate([base, 0.8 * jnp.roll(base, 1, axis=2)], axis=-1)[..., :COUT]
    field = (0.6 * paired + noise) * position_scale()
    return field.reshape(SAMPLES, NX, NY, NZ * COUT).astype(jnp.bfloat16)


def draw_a_inverse(key, part):
    key = jax.random.fold_in(key, 7)
    return symmetric_matrix(key, KC, 0.5, 2.0)


def draw_g_inverse(key, part):
    key = jax.random.fold_in(key, 9)
    return symmetric_matrix(key, COUT, 0.5, 2.0)


def gaussian(rng, extent, scale, most, kind=jnp.bfloat16):
    values = scale * jax.random.normal(rng, extent, jnp.float32)
    return jnp.clip(values, min=-most, max=most).astype(kind)


def setup_inputs(seed: int = 0) -> dict:
    splits = jax.random.split(jax.random.key(seed), 6)
    activations = draw_activations(jax.random.fold_in(splits[5], 71), 0)
    cotangent = draw_cotangent(jax.random.fold_in(splits[5], 71), 0)
    weight = gaussian(splits[2], (COUT, KC), KC ** -0.5, 0.15625)
    a_inverse = draw_a_inverse(jax.random.fold_in(splits[5], 71), 0)
    g_inverse = draw_g_inverse(jax.random.fold_in(splits[5], 71), 0)
    return {"activations": activations, "cotangent": cotangent, "weight": weight, "a_inverse": a_inverse, "g_inverse": g_inverse}


def grid_patches(extended, planes, span_y, span_z, chans, mirror):
    volume = extended.reshape(planes + 2, span_y, span_z, chans)
    volume = jnp.pad(volume, ((0, 0), (1, 1), (1, 1), (0, 0)))
    pieces = []
    for shift_x in range(3):
        for shift_y in range(3):
            for shift_z in range(3):
                start_x = 2 - shift_x if mirror else shift_x
                start_y = 2 - shift_y if mirror else shift_y
                start_z = 2 - shift_z if mirror else shift_z
                pieces.append(volume[start_x:start_x + planes, start_y:start_y + span_y, start_z:start_z + span_z, :])
    return jnp.concatenate(pieces, axis=-1).reshape(planes * span_y * span_z, 27 * chans)


def contract(left, right):
    return lax.dot_general(left, right, (((0,), (0,)), ((), ())), preferred_element_type=jnp.float32)


def reference(activations, cotangent, weight, a_inverse, g_inverse):
    flipped = weight.reshape(COUT, 27, CIN).transpose(1, 0, 2).reshape(27 * COUT, CIN)

    def per_sample(running, slices):
        field, grad_field = slices
        patches = grid_patches(jnp.pad(field, ((1, 1), (0, 0), (0, 0))), NX, NY, NZ, CIN, False)
        result = jnp.dot(patches, weight.T, preferred_element_type=jnp.float32).astype(jnp.bfloat16)
        grad_patches = grid_patches(jnp.pad(grad_field, ((1, 1), (0, 0), (0, 0))), NX, NY, NZ, COUT, True)
        backward = jnp.dot(grad_patches, flipped, preferred_element_type=jnp.float32).astype(jnp.bfloat16)
        flat_grad = grad_field.reshape(NX * NY * NZ, COUT)
        a_sum, g_sum, w_sum = running
        a_sum = a_sum + contract(patches, patches)
        g_sum = g_sum + contract(flat_grad, flat_grad)
        w_sum = w_sum + contract(flat_grad, patches)
        return (a_sum, g_sum, w_sum), (result.reshape(NX, NY, NZ * COUT), backward.reshape(NX, NY, NZ * CIN))

    start_sums = (jnp.zeros((KC, KC), jnp.float32), jnp.zeros((COUT, COUT), jnp.float32), jnp.zeros((COUT, KC), jnp.float32))
    sums, results = lax.scan(per_sample, start_sums, (activations, cotangent))
    a_sum, g_sum, w_sum = sums
    outputs, input_grad = results
    cell_total = float(SAMPLES * NX * NY * NZ)
    a_factor = a_sum / cell_total
    g_factor = g_sum / cell_total
    grad = w_sum / cell_total
    half_step = jnp.dot(grad, a_inverse, precision=lax.Precision.HIGHEST)
    update = jnp.dot(g_inverse, half_step, precision=lax.Precision.HIGHEST)
    return outputs, input_grad, a_factor, g_factor, update
```

```python
import jax
import jax.numpy as jnp
from jax import lax
from jax.experimental import pallas as pl
from jax.experimental.pallas import tpu as pltpu
from jax.sharding import PartitionSpec as P

MESH = pl.DeviceIdType.MESH
F32 = jnp.float32
BF16 = jnp.bfloat16

CIN, COUT = 64, 128
NY, NZ = 8, 16
CELLS = NY * NZ
KC = 27 * CIN
ROWS = 9 * CIN
SHARE = KC // 32
HALF = 896
PLANES = 34
TOTAL = float(8 * 64 * CELLS)

Z_DELTAS = (1, 7, 2, 6, 3, 5, 4)
XY_DELTAS = tuple(
    sorted(
        ((a, b) for a in range(4) for b in range(4) if (a, b) != (0, 0)),
        key=lambda d: -(min(d[0], 4 - d[0]) + min(d[1], 4 - d[1])),
    )
)
SAMPLE_DELTAS = tuple(d for d in XY_DELTAS if d[0] % 2 == 0)


def nt(left, right):
    return lax.dot_general(left, right, (((1,), (1,)), ((), ())), preferred_element_type=F32)


def nn(left, right):
    return lax.dot_general(left, right, (((1,), (0,)), ((), ())), preferred_element_type=F32)


def tn(left, right):
    return lax.dot_general(left, right, (((0,), (0,)), ((), ())), preferred_element_type=F32)


def aligned(value, unit):
    return pl.multiple_of(value, unit)


def step_kernel(
    act_hbm, cot_hbm, weight_hbm, ainv_hbm,
    fin_ref, out_ref, igrad_ref, half_ref,
    planes, shifted, shift01, chosen, acc, rows_tmp, cells_tmp, cot_t, act_ref, cot_ref, weight_t, ainv_ref, load,
    send_a, recv_a, fin, send_g, recv_g, zsend, zrecv, quarters, hg,
    z_s, z_r, f_s, f_r, b_s, b_r, bf_s, bf_r, c_s, c_r,
    g_s, g_r, q_s, q_r, k_s, k_r, u_s, u_r, a_s, a_r, v_s, v_r,
):
    j = lax.axis_index("sample")
    s = lax.axis_index("space")
    xh, y = j // 4, j % 4
    xl, z, core = s // 16, (s // 2) % 8, s % 2
    x = xh * 2 + xl

    def dev(dx=0, dy=0, dz=0, other=False):
        x2, y2, z2 = (x + dx) % 4, (y + dy) % 4, (z + dz) % 8
        c2 = 1 - core if other else core
        return {"sample": (x2 // 2) * 4 + y2, "space": ((x2 % 2) * 8 + z2) * 2 + c2}

    def at_space(s2):
        return {"sample": j, "space": s2}

    def copy(src, dst, ssem, rsem, device):
        return pltpu.make_async_remote_copy(
            src_ref=src, dst_ref=dst, send_sem=ssem, recv_sem=rsem,
            device_id=device, device_id_type=MESH,
        )

    across = at_space((s + 32 - 1 + 2 * core) % 32)
    xl_peer = at_space(((1 - xl) * 8 + z) * 2 + core)
    xl_other = at_space(((1 - xl) * 8 + z) * 2 + 1 - core)
    edge_sender = jnp.logical_and(z == 7 * (1 - xl), core == 1 - xl)
    edge_receiver = core == xl
    edge_slot = 33 * (1 - xl)
    near_edge = z == 7 * (1 - xl)

    loads = [
        pltpu.make_async_copy(src, dst, load.at[n])
        for n, (src, dst) in enumerate(
            ((act_hbm, act_ref), (cot_hbm, cot_ref), (weight_hbm, weight_t), (ainv_hbm, ainv_ref))
        )
    ]
    for c in loads:
        c.start()

    barrier = pltpu.get_barrier_semaphore()

    def greet(device):
        pl.semaphore_signal(barrier, inc=1, device_id=device, device_id_type=MESH)

    for d in Z_DELTAS:
        greet(dev(dz=d))
    for dx, dy in XY_DELTAS:
        greet(dev(dx, dy))
    greet(dev(other=True))
    greet(xl_other)
    greet(across)

    @pl.when(edge_receiver)
    def _():
        greet(at_space(((1 - xl) * 8 + 7 * xl) * 2 + core))

    mine = 1 + 4 * z + 2 * core
    loads[0].wait()
    loads[1].wait()
    for p in range(2):
        for zz in range(NZ):
            pair = act_ref[p, :, (zz // 2) * 128 : (zz // 2) * 128 + 128].astype(F32)
            if zz % 2:
                pair = pltpu.roll(pair, 64, 1)
            cells_tmp[p, pl.ds(zz, NY, stride=NZ), :] = pair
    for p in range(2):
        for zz in range(NZ):
            cells_tmp[2 + p, pl.ds(zz, NY, stride=NZ), :] = cot_ref[
                p, :, zz * 128 : zz * 128 + 128
            ].astype(F32)
    for p in range(2):
        planes[mine + p] = jnp.transpose(cells_tmp[p])[:CIN].astype(BF16)
        cot_t[1 + 2 * core + p] = jnp.transpose(cells_tmp[2 + p]).astype(BF16)

    src = lax.broadcasted_iota(jnp.int32, (CELLS, CELLS), 0)
    cell = lax.broadcasted_iota(jnp.int32, (CELLS, CELLS), 1)
    cy, cz = cell // NZ, cell % NZ
    for n in range(9):
        dy, dz = n // 3 - 1, n % 3 - 1
        inside = (cy + dy >= 0) & (cy + dy < NY) & (cz + dz >= 0) & (cz + dz < NZ)
        hit = inside & (src == cell + dy * NZ + dz)
        shift01[:, n * CELLS : (n + 1) * CELLS] = jnp.where(hit, 1.0, 0.0).astype(BF16)

    planes[33 * xl] = jnp.zeros((CIN, CELLS), BF16)

    def build(first, count):
        value = planes[pl.ds(first, count)].reshape(count * CIN, CELLS)
        moved = nn(value, shift01[...]).astype(BF16)
        for q in range(count):
            for n in range(9):
                shifted[pl.ds(aligned((first + q) * ROWS + n * CIN, 64), CIN), :] = moved[
                    q * CIN : (q + 1) * CIN, n * CELLS : (n + 1) * CELLS
                ]

    def put(first, count, ssem, rsem, device):
        ref = planes.at[pl.ds(first, count)]
        return copy(ref, ref, ssem, rsem, device)

    peers = len(Z_DELTAS) + len(XY_DELTAS) + 3
    pl.semaphore_wait(barrier, peers + jnp.where(edge_sender, 8, 0))

    cot_core = copy(
        cot_t.at[pl.ds(1 + 2 * core, 2)], cot_t.at[pl.ds(1 + 2 * core, 2)],
        c_s.at[0], c_r.at[0], dev(other=True),
    )
    cot_edge = copy(
        cot_t.at[1 + 3 * core], cot_t.at[5 * (1 - core)], c_s.at[1], c_r.at[1], across
    )
    z_out = []
    for n, d in enumerate(Z_DELTAS):
        z_out.append(put(mine, 2, z_s.at[n], z_r.at[n], dev(dz=d)))
    f_out = [put(mine, 2, f_s.at[0], f_r.at[0], dev(other=True))]

    def edge_copy(i):
        zz = (z + i) % 8
        return copy(
            planes.at[32 - 31 * xl], planes.at[33 * xl],
            b_s.at[i], b_r.at[0], at_space(((1 - xl) * 8 + zz) * 2 + core),
        )

    edge_order = (1, 0, 7, 2, 6, 3, 5, 4)
    f_out[0].start()
    z_out[0].start()
    z_out[1].start()

    @pl.when(edge_sender)
    def _():
        for i in edge_order:
            edge_copy(i).start()

    for c in z_out[2:]:
        c.start()
    cot_core.start()
    cot_edge.start()

    edge_forward = put(edge_slot, 1, bf_s.at[0], bf_r.at[0], dev(other=True))

    def edge_arrive():
        @pl.when(edge_receiver)
        def _():
            edge_copy(0).wait_recv()
            edge_forward.start()

        @pl.when(jnp.logical_not(edge_receiver))
        def _():
            edge_forward.wait_recv()

        build(edge_slot, 1)

    def from_chip(n):
        return 1 + 4 * ((z + 8 - Z_DELTAS[n]) % 8)

    def arrive(n):
        z_out[n].wait_recv()
        c = put(from_chip(n) + 2 * core, 2, f_s.at[n + 1], f_r.at[n + 1], dev(other=True))
        c.start()
        f_out.append(c)

    build(33 * xl, 1)
    build(mine, 2)
    f_out[0].wait_recv()
    build(1 + 4 * z + 2 * (1 - core), 2)
    arrive(0)
    arrive(1)
    build(from_chip(0) + 2 * core, 2)
    build(from_chip(1) + 2 * core, 2)
    f_out[1].wait_recv()
    f_out[2].wait_recv()
    build(from_chip(0) + 2 * (1 - core), 2)
    build(from_chip(1) + 2 * (1 - core), 2)

    @pl.when(near_edge)
    def _():
        edge_arrive()

    cot_core.wait_recv()
    cot_cat = jnp.concatenate([cot_t[1], cot_t[2], cot_t[3], cot_t[4]], axis=1)

    def patch_cat(first, offset):
        return jnp.concatenate(
            [
                shifted[pl.ds(aligned((first + i - 1) * ROWS + offset, 64), HALF), :]
                for i in range(4)
            ],
            axis=1,
        )

    w_part = nt(cot_cat, patch_cat(4 * z + 1, core * HALF)).astype(BF16)
    g_part = nt(cot_cat, cot_cat).astype(BF16)
    for r in range(8):
        send_g[0, r] = w_part[r * 16 : r * 16 + 16, :512]
        send_g[1, r, :, :384] = w_part[r * 16 : r * 16 + 16, 512:]
        send_g[1, r, :, 384:] = g_part[r * 16 : r * 16 + 16]
    g_out = []
    for n, (dx, dy) in enumerate(XY_DELTAS):
        x2, y2 = (x + dx) % 4, (y + dy) % 4
        c = copy(
            send_g.at[x2 % 2, (x2 // 2) * 4 + y2], recv_g.at[n],
            g_s.at[n], g_r.at[n], dev(dx, dy),
        )
        c.start()
        g_out.append(c)

    for n in range(2, 7):
        arrive(n)
        build(from_chip(n) + 2 * core, 2)
    for n in range(2, 7):
        f_out[n + 1].wait_recv()
        build(from_chip(n) + 2 * (1 - core), 2)

    @pl.when(jnp.logical_not(near_edge))
    def _():
        edge_arrive()

    first_row = SHARE * (2 * z + core)
    base = (first_row // 16) * 16
    off = first_row % 16

    def choose(i, carry):
        for t in range(2):
            start = aligned(i * ROWS + t * 16 * SHARE + base, 16)
            rows_tmp[t] = shifted[pl.ds(start, 80), :].astype(F32)
            chosen[i, t * 64 : t * 64 + 64, :] = rows_tmp[t, pl.ds(off, 64), :].astype(BF16)
        return carry

    lax.fori_loop(0, 32, choose, 0)

    a_out = []

    def covariance(h):
        def body(i, carry):
            left = jnp.concatenate([chosen[4 * i + q] for q in range(4)], axis=1)
            acc[h] += nt(left, patch_cat(4 * i + 1, h * HALF))
            return carry

        acc[h] = jnp.zeros((128, HALF), F32)
        lax.fori_loop(0, 8, body, 0)
        for t in range(2):
            for q in range(4):
                send_a[t, 2 * q + h] = acc[h, t * 64 + q * 16 : t * 64 + q * 16 + 16].astype(BF16)

    covariance(0)
    covariance(1)
    for n, (dx, dy) in enumerate(XY_DELTAS):
        x2, y2 = (x + dx) % 4, (y + dy) % 4
        c = copy(
            send_a.at[x2 % 2, (x2 // 2) * 4 + y2], recv_a.at[n],
            a_s.at[n], a_r.at[n], dev(dx, dy),
        )
        c.start()
        a_out.append(c)

    total = send_g[xl, j].astype(F32)
    for n in range(15):
        g_out[n].wait_recv()
        total += recv_g[n].astype(F32)
    zsend[...] = total.astype(BF16)
    q_out = []
    for n, d in enumerate(Z_DELTAS):
        c = copy(zsend, zrecv.at[n], q_s.at[n], q_r.at[n], dev(dz=d))
        c.start()
        q_out.append(c)

    loads[2].wait()
    for p in range(2):
        patch = shifted[pl.ds(aligned((mine + p - 1) * ROWS, 64), KC), :]
        cells_tmp[p] = tn(patch, weight_t[...])
    for p in range(2):
        for zz in range(NZ):
            out_ref[p, :, zz * 128 : zz * 128 + 128] = cells_tmp[
                p, pl.ds(zz, NY, stride=NZ), :
            ].astype(BF16)

    cot_edge.wait_recv()

    @pl.when(s == 0)
    def _():
        cot_t[0] = jnp.zeros((COUT, CELLS), BF16)

    @pl.when(s == 31)
    def _():
        cot_t[5] = jnp.zeros((COUT, CELLS), BF16)

    w_cat = jnp.concatenate([weight_t[r * ROWS : (r + 1) * ROWS, :] for r in range(3)], axis=1)
    c64 = lax.broadcasted_iota(jnp.int32, (CIN, CELLS), 1)
    ly, lz = c64 // NZ, c64 % NZ
    for p in range(2):
        here = 1 + 2 * core + p
        c_cat = jnp.concatenate([cot_t[here + 1], cot_t[here], cot_t[here - 1]], axis=0)
        spread = nn(w_cat, c_cat)
        back = jnp.zeros((CIN, CELLS), F32)
        for n in range(9):
            dy, dz = n // 3 - 1, n % 3 - 1
            part = spread[n * CIN : (n + 1) * CIN]
            turn = (dy * NZ + dz) % CELLS
            if turn:
                part = pltpu.roll(part, turn, 1)
            inside = (ly - dy >= 0) & (ly - dy < NY) & (lz - dz >= 0) & (lz - dz < NZ)
            back += jnp.where(inside, part, 0.0)
        cells_tmp[2 + p] = jnp.transpose(jnp.concatenate([back, back], axis=0))
    lane = lax.broadcasted_iota(jnp.int32, (NY, 128), 1)
    for p in range(2):
        for zp in range(NZ // 2):
            even = cells_tmp[2 + p, pl.ds(2 * zp, NY, stride=NZ), :]
            odd = cells_tmp[2 + p, pl.ds(2 * zp + 1, NY, stride=NZ), :]
            igrad_ref[p, :, zp * 128 : zp * 128 + 128] = jnp.where(lane < 64, even, odd).astype(BF16)

    total = zsend[...].astype(F32)
    for n in range(7):
        q_out[n].wait_recv()
        total += zrecv[n].astype(F32)
    quarter = core * 2 + xl
    quarters[quarter] = total.astype(BF16)
    k_out = []
    for n, (device, other) in enumerate(
        ((xl_other, 3 - quarter), (xl_peer, core * 2 + 1 - xl), (dev(other=True), (1 - core) * 2 + xl))
    ):
        c = copy(quarters.at[quarter], quarters.at[quarter], k_s.at[n], k_r.at[n], device)
        c.start()
        k_out.append(c)
    loads[3].wait()
    ainv = ainv_ref[...]
    a_hi = ainv.astype(BF16)
    a_lo = (ainv - a_hi.astype(F32)).astype(BF16)

    piece = send_a[xl, j].astype(F32)
    for n in range(15):
        a_out[n].wait_recv()
        piece += recv_a[n].astype(F32)
    fin[j] = (piece * (1.0 / TOTAL)).astype(BF16)
    v_out = []
    for n, (dx, dy) in enumerate(SAMPLE_DELTAS):
        c = copy(fin.at[j], fin.at[j], v_s.at[n], v_r.at[n], dev(dx, dy))
        c.start()
        v_out.append(c)

    for c in k_out:
        c.wait_recv()
    grad = jnp.concatenate(
        [quarters[0], quarters[1, :, :384], quarters[2], quarters[3, :, :384]], axis=1
    )[:, :KC]
    half = (nt(grad, a_hi) + nt(grad, a_lo)) * (1.0 / TOTAL)
    hg[j, :, :128] = jnp.concatenate([half, jnp.zeros((16, 128 - SHARE), F32)], axis=1).astype(BF16)
    hg[j, :, 128:] = quarters[1, :, 384:]
    u_out = []
    for n, (dx, dy) in enumerate(SAMPLE_DELTAS):
        c = copy(hg.at[j], hg.at[j], u_s.at[n], u_r.at[n], dev(dx, dy))
        c.start()
        u_out.append(c)

    for c in v_out:
        c.wait_recv()
    fin_ref[...] = fin[...]
    for c in u_out:
        c.wait_recv()
    half_ref[...] = hg[...]

    for c in z_out + f_out + [cot_core, cot_edge] + g_out + q_out + k_out + a_out + v_out + u_out:
        c.wait_send()

    @pl.when(edge_receiver)
    def _():
        edge_forward.wait_send()

    @pl.when(edge_sender)
    def _():
        for i in range(8):
            edge_copy(i).wait_send()


def finish_kernel(
    fin_ref, out_in, igrad_in, hg_ref, ginv_ref, out_ref, igrad_ref, a_ref, g_ref, update_ref
):
    out_ref[...] = out_in[...]
    igrad_ref[...] = igrad_in[...]
    for q in range(4):
        deep = min(16, SHARE - 16 * q)
        a_ref[16 * q : 16 * q + deep, :HALF] = fin_ref[2 * q][:deep].astype(F32)
        a_ref[16 * q : 16 * q + deep, HALF:] = fin_ref[2 * q + 1][:deep, : KC - HALF].astype(F32)
    hg = hg_ref[...].reshape(COUT, 256)
    g_ref[...] = hg[:, 128:].astype(F32) * (1.0 / TOTAL)
    update = lax.dot_general(
        ginv_ref[...], hg[:, :128].astype(F32), (((1,), (0,)), ((), ())),
        precision=lax.Precision.HIGHEST, preferred_element_type=F32,
    )
    update_ref[...] = jnp.transpose(update)[:SHARE]


def shards(activations, cotangent, weight, a_inverse, g_inverse):
    vmem = pl.BlockSpec(memory_space=pltpu.VMEM)
    dma = pltpu.SemaphoreType.DMA
    counts = (7, 7, 8, 8, 8, 1, 1, 1, 2, 2, 15, 15, 7, 7, 3, 3, 7, 7, 15, 15, 7, 7)
    fin, outs, igrad, hg = pl.pallas_call(
        step_kernel,
        out_shape=(
            jax.ShapeDtypeStruct((8, 16, HALF), BF16),
            jax.ShapeDtypeStruct((2, NY, NZ * COUT), BF16),
            jax.ShapeDtypeStruct((2, NY, NZ * CIN), BF16),
            jax.ShapeDtypeStruct((8, 16, 256), BF16),
        ),
        in_specs=[pl.BlockSpec(memory_space=pltpu.HBM)] * 4,
        out_specs=[vmem] * 4,
        scratch_shapes=[
            pltpu.VMEM((PLANES, CIN, CELLS), BF16),
            pltpu.VMEM(((PLANES + 1) * ROWS, CELLS), BF16),
            pltpu.VMEM((CELLS, 9 * CELLS), BF16),
            pltpu.VMEM((32, 128, CELLS), BF16),
            pltpu.VMEM((2, 128, HALF), F32),
            pltpu.VMEM((2, 80, CELLS), F32),
            pltpu.VMEM((4, CELLS, 128), F32),
            pltpu.VMEM((6, COUT, CELLS), BF16),
            pltpu.VMEM((2, NY, NZ * CIN), BF16),
            pltpu.VMEM((2, NY, NZ * COUT), BF16),
            pltpu.VMEM((KC, COUT), BF16),
            pltpu.VMEM((SHARE, KC), F32),
            dma((4,)),
            pltpu.VMEM((2, 8, 16, HALF), BF16),
            pltpu.VMEM((15, 16, HALF), BF16),
            pltpu.VMEM((8, 16, HALF), BF16),
            pltpu.VMEM((2, 8, 16, 512), BF16),
            pltpu.VMEM((15, 16, 512), BF16),
            pltpu.VMEM((16, 512), BF16),
            pltpu.VMEM((7, 16, 512), BF16),
            pltpu.VMEM((4, 16, 512), BF16),
            pltpu.VMEM((8, 16, 256), BF16),
        ]
        + [dma((n,)) for n in counts],
        compiler_params=pltpu.CompilerParams(
            collective_id=0, has_side_effects=True, vmem_limit_bytes=63 << 20
        ),
        cost_estimate=pl.CostEstimate(flops=2 * 10**9, bytes_accessed=2 * 10**6, transcendentals=0),
        name="step",
    )(activations[0], cotangent[0], weight.T, a_inverse)
    outputs, input_grad, a_factor, g_factor, update = pl.pallas_call(
        finish_kernel,
        out_shape=(
            jax.ShapeDtypeStruct((2, NY, NZ * COUT), BF16),
            jax.ShapeDtypeStruct((2, NY, NZ * CIN), BF16),
            jax.ShapeDtypeStruct((SHARE, KC), F32),
            jax.ShapeDtypeStruct((COUT, COUT), F32),
            jax.ShapeDtypeStruct((SHARE, COUT), F32),
        ),
        in_specs=[vmem] * 5,
        out_specs=[vmem] * 5,
        compiler_params=pltpu.CompilerParams(vmem_limit_bytes=63 << 20),
        name="finish",
    )(fin, outs, igrad, hg, g_inverse)
    return outputs[None], input_grad[None], a_factor, g_factor, update.T


def solution(mesh):
    return jax.shard_map(
        shards,
        mesh=mesh,
        in_specs=(
            P("sample", "space", None, None),
            P("sample", "space", None, None),
            P(),
            P("space", None),
            P(),
        ),
        out_specs=(
            P("sample", "space", None, None),
            P("sample", "space", None, None),
            P("space", None),
            P(),
            P(None, "space"),
        ),
        check_vma=False,
    )
```

```python
import jax
import jax.numpy as jnp
from jax import lax
from jax.experimental import pallas as pl
from jax.experimental.pallas import tpu as pltpu
from jax.sharding import PartitionSpec as P

MESH = pl.DeviceIdType.MESH
F32 = jnp.float32
BF16 = jnp.bfloat16

CIN, COUT = 64, 128
NY, NZ = 8, 16
CELLS = NY * NZ
KC = 27 * CIN
ROWS = 9 * CIN
SHARE = KC // 32
HALF = 896
PLANES = 34
TOTAL = float(8 * 64 * CELLS)

Z_DELTAS = (1, 7, 2, 6, 3, 5, 4)
XY_DELTAS = tuple(
    sorted(
        ((a, b) for a in range(4) for b in range(4) if (a, b) != (0, 0)),
        key=lambda d: -(min(d[0], 4 - d[0]) + min(d[1], 4 - d[1])),
    )
)
SAMPLE_DELTAS = tuple(d for d in XY_DELTAS if d[0] % 2 == 0)


def nt(left, right):
    return lax.dot_general(left, right, (((1,), (1,)), ((), ())), preferred_element_type=F32)


def nn(left, right):
    return lax.dot_general(left, right, (((1,), (0,)), ((), ())), preferred_element_type=F32)


def tn(left, right):
    return lax.dot_general(left, right, (((0,), (0,)), ((), ())), preferred_element_type=F32)


def aligned(value, unit):
    return pl.multiple_of(value, unit)


def step_kernel(
    act_hbm, cot_hbm, weight_hbm, ainv_hbm,
    fin_ref, out_ref, igrad_ref, half_ref,
    planes, shifted, chosen, acc, side, rows_tmp, cells_tmp, cot_t, act_ref, cot_ref, weight_t, ainv_ref, load,
    send_a, recv_a, fin, send_g, recv_g, zsend, zrecv, quarters, hg,
    z_s, z_r, f_s, f_r, b_s, b_r, bf_s, bf_r, c_s, c_r,
    g_s, g_r, q_s, q_r, k_s, k_r, u_s, u_r, a_s, a_r, v_s, v_r,
):
    j = lax.axis_index("sample")
    s = lax.axis_index("space")
    xh, y = j // 4, j % 4
    xl, z, core = s // 16, (s // 2) % 8, s % 2
    x = xh * 2 + xl

    def dev(dx=0, dy=0, dz=0, other=False):
        x2, y2, z2 = (x + dx) % 4, (y + dy) % 4, (z + dz) % 8
        c2 = 1 - core if other else core
        return {"sample": (x2 // 2) * 4 + y2, "space": ((x2 % 2) * 8 + z2) * 2 + c2}

    def at_space(s2):
        return {"sample": j, "space": s2}

    def copy(src, dst, ssem, rsem, device):
        return pltpu.make_async_remote_copy(
            src_ref=src, dst_ref=dst, send_sem=ssem, recv_sem=rsem,
            device_id=device, device_id_type=MESH,
        )

    across = at_space((s + 32 - 1 + 2 * core) % 32)
    xl_peer = at_space(((1 - xl) * 8 + z) * 2 + core)
    xl_other = at_space(((1 - xl) * 8 + z) * 2 + 1 - core)
    edge_sender = jnp.logical_and(z == 7 * (1 - xl), core == 1 - xl)
    edge_receiver = core == xl
    edge_slot = 33 * (1 - xl)
    edge_far = jnp.minimum((z + 1 - xl) % 8, (7 * (1 - xl) + 8 - z) % 8)
    edge_far = jnp.minimum(edge_far, 3)

    loads = [
        pltpu.make_async_copy(src, dst, load.at[n])
        for n, (src, dst) in enumerate(
            ((act_hbm, act_ref), (cot_hbm, cot_ref), (weight_hbm, weight_t), (ainv_hbm, ainv_ref))
        )
    ]
    for c in loads:
        c.start()

    barrier = pltpu.get_barrier_semaphore()

    def greet(device):
        pl.semaphore_signal(barrier, inc=1, device_id=device, device_id_type=MESH)

    for d in Z_DELTAS:
        greet(dev(dz=d))
    for dx, dy in XY_DELTAS:
        greet(dev(dx, dy))
    greet(dev(other=True))
    greet(xl_other)
    greet(across)

    @pl.when(edge_receiver)
    def _():
        greet(at_space(((1 - xl) * 8 + 7 * xl) * 2 + core))

    mine = 1 + 4 * z + 2 * core
    loads[0].wait()
    loads[1].wait()
    for p in range(2):
        for zz in range(NZ):
            pair = act_ref[p, :, (zz // 2) * 128 : (zz // 2) * 128 + 128].astype(F32)
            if zz % 2:
                pair = pltpu.roll(pair, 64, 1)
            cells_tmp[p, pl.ds(zz, NY, stride=NZ), :] = pair
    for p in range(2):
        for zz in range(NZ):
            cells_tmp[2 + p, pl.ds(zz, NY, stride=NZ), :] = cot_ref[
                p, :, zz * 128 : zz * 128 + 128
            ].astype(F32)
    for p in range(2):
        planes[mine + p] = jnp.transpose(cells_tmp[p])[:CIN].astype(BF16)
        cot_t[1 + 2 * core + p] = jnp.transpose(cells_tmp[2 + p]).astype(BF16)

    lane = lax.broadcasted_iota(jnp.int32, (CIN, CELLS), 1)
    ly, lz = lane // NZ, lane % NZ

    def within(dy, dz):
        return (ly + dy >= 0) & (ly + dy < NY) & (lz + dz >= 0) & (lz + dz < NZ)

    planes[33 * xl] = jnp.zeros((CIN, CELLS), BF16)

    def build_from(value, i):
        for n in range(9):
            dy, dz = n // 3 - 1, n % 3 - 1
            turn = -(dy * NZ + dz) % CELLS
            moved = pltpu.roll(value, turn, 1) if turn else value
            shifted[pl.ds(aligned(i * ROWS + n * CIN, 64), CIN), :] = jnp.where(
                within(dy, dz), moved, 0.0
            ).astype(BF16)

    def build(first, count):
        for q in range(count):
            build_from(planes[first + q].astype(F32), first + q)

    def put(first, count, ssem, rsem, device):
        ref = planes.at[pl.ds(first, count)]
        return copy(ref, ref, ssem, rsem, device)

    peers = len(Z_DELTAS) + len(XY_DELTAS) + 3
    pl.semaphore_wait(barrier, peers + jnp.where(edge_sender, 8, 0))

    cot_core = copy(
        cot_t.at[pl.ds(1 + 2 * core, 2)], cot_t.at[pl.ds(1 + 2 * core, 2)],
        c_s.at[0], c_r.at[0], dev(other=True),
    )
    cot_edge = copy(
        cot_t.at[1 + 3 * core], cot_t.at[5 * (1 - core)], c_s.at[1], c_r.at[1], across
    )
    side_copy = copy(planes.at[mine + core], side, c_s.at[2], c_r.at[2], across)
    z_out = []
    for n, d in enumerate(Z_DELTAS):
        z_out.append(put(mine, 2, z_s.at[n], z_r.at[n], dev(dz=d)))
    f_out = [put(mine, 2, f_s.at[0], f_r.at[0], dev(other=True))]

    def edge_copy(i):
        zz = (z + i) % 8
        return copy(
            planes.at[32 - 31 * xl], planes.at[33 * xl],
            b_s.at[i], b_r.at[0], at_space(((1 - xl) * 8 + zz) * 2 + core),
        )

    edge_order = (1, 0, 7, 2, 6, 3, 5, 4)
    z_out[0].start()
    z_out[1].start()
    side_copy.start()
    f_out[0].start()
    cot_core.start()

    @pl.when(edge_sender)
    def _():
        for i in edge_order:
            edge_copy(i).start()

    for c in z_out[2:]:
        c.start()
    cot_edge.start()

    edge_forward = put(edge_slot, 1, bf_s.at[0], bf_r.at[0], dev(other=True))

    def edge_arrive(level):
        @pl.when(jnp.logical_and(edge_receiver, edge_far == level))
        def _():
            edge_copy(0).wait_recv()
            edge_forward.start()
            build(edge_slot, 1)

        @pl.when(jnp.logical_and(jnp.logical_not(edge_receiver), jnp.maximum(edge_far, 1) == level))
        def _():
            edge_forward.wait_recv()
            build(edge_slot, 1)

    def from_chip(n):
        return 1 + 4 * ((z + 8 - Z_DELTAS[n]) % 8)

    def arrive(n):
        z_out[n].wait_recv()
        c = put(from_chip(n) + 2 * core, 2, f_s.at[n + 1], f_r.at[n + 1], dev(other=True))
        c.start()
        f_out.append(c)

    build(33 * xl, 1)
    build(mine, 2)
    f_out[0].wait_recv()
    build(1 + 4 * z + 2 * (1 - core), 2)
    arrive(0)
    arrive(1)
    beside = 4 * z + 5 * (1 - core)

    @pl.when(jnp.logical_and(beside > 0, beside < 33))
    def _():
        build(beside, 1)

    side_copy.wait_recv()

    @pl.when(jnp.logical_and(s > 0, s < 31))
    def _():
        build_from(side[...].astype(F32), 4 * z + 5 * core)

    edge_arrive(0)

    cot_core.wait_recv()
    cot_cat = jnp.concatenate([cot_t[1], cot_t[2], cot_t[3], cot_t[4]], axis=1)

    def patch_cat(first, offset):
        return jnp.concatenate(
            [
                shifted[pl.ds(aligned((first + i - 1) * ROWS + offset, 64), HALF), :]
                for i in range(4)
            ],
            axis=1,
        )

    w_part = nt(cot_cat, patch_cat(4 * z + 1, core * HALF)).astype(BF16)
    g_part = nt(cot_cat, cot_cat).astype(BF16)
    for r in range(8):
        send_g[0, r] = w_part[r * 16 : r * 16 + 16, :512]
        send_g[1, r, :, :384] = w_part[r * 16 : r * 16 + 16, 512:]
        send_g[1, r, :, 384:] = g_part[r * 16 : r * 16 + 16]
    g_out = []
    for n, (dx, dy) in enumerate(XY_DELTAS):
        x2, y2 = (x + dx) % 4, (y + dy) % 4
        c = copy(
            send_g.at[x2 % 2, (x2 // 2) * 4 + y2], recv_g.at[n],
            g_s.at[n], g_r.at[n], dev(dx, dy),
        )
        c.start()
        g_out.append(c)

    first_row = SHARE * (2 * z + core)
    base = (first_row // 16) * 16
    off = first_row % 16

    def choose(i, carry):
        for t in range(2):
            start = aligned((i - 1) * ROWS + t * 16 * SHARE + base, 16)
            rows_tmp[t] = shifted[pl.ds(start, 80), :].astype(F32)
            chosen[i, t * 64 : t * 64 + 64, :] = rows_tmp[t, pl.ds(off, 64), :].astype(BF16)
        return carry

    chosen[0] = jnp.zeros((128, CELLS), BF16)
    chosen[33] = jnp.zeros((128, CELLS), BF16)

    def covariance(chips, fresh=False):
        for chip in chips:
            for i in range(6):
                choose(jnp.clip(4 * chip + i, 1, 32), 0)
        spots = [4 * chip + 1 + q for chip in chips for q in range(4)]
        left = jnp.concatenate(
            [shifted[pl.ds(aligned(i * ROWS, 64), ROWS), :] for i in spots], axis=1
        )
        right = jnp.concatenate(
            [jnp.concatenate([chosen[i - k] for i in spots], axis=1) for k in (-1, 0, 1)], axis=0
        )
        if fresh:
            acc[...] = nt(left, right)
        else:
            acc[...] += nt(left, right)

    for n in range(2):
        build(from_chip(n) + 2 * core, 2)
    for n in range(2):
        f_out[n + 1].wait_recv()
        build(from_chip(n) + 2 * (1 - core), 2)
    covariance((z,), fresh=True)
    for level in (1, 2, 3):
        news = (2, 3) if level == 1 else (4, 5) if level == 2 else (6,)
        for n in news:
            arrive(n)
            build(from_chip(n) + 2 * core, 2)
        for n in news:
            f_out[n + 1].wait_recv()
            build(from_chip(n) + 2 * (1 - core), 2)

        edge_arrive(level)
        near = ((z + 8 - level) % 8, (z + level) % 8)
        covariance(near if level < 3 else near + ((z + 4) % 8,))

    @pl.when(xl == 0)
    def _():
        acc[:, 256:] += nt(shifted[33 * ROWS : 34 * ROWS, :], chosen[32])

    @pl.when(xl == 1)
    def _():
        acc[:, :128] += nt(shifted[:ROWS, :], chosen[1])

    def column_tile(k):
        parts = []
        start, stop = 128 * k, min(128 * k + 128, KC)
        while start < stop:
            kx, row = start // ROWS, start % ROWS
            deep = min(stop - start, ROWS - row)
            parts.append(acc[row : row + deep, kx * 128 : kx * 128 + 128])
            start += deep
        return jnp.transpose(jnp.concatenate(parts, axis=0)).astype(BF16)

    a_out = []
    for n, (dx, dy) in enumerate(XY_DELTAS):
        x2, y2 = (x + dx) % 4, (y + dy) % 4
        a_out.append(
            copy(
                send_a.at[x2 % 2, (x2 // 2) * 4 + y2], recv_a.at[n],
                a_s.at[n], a_r.at[n], dev(dx, dy),
            )
        )
    for h in range(2):
        for k in range(7):
            tile = column_tile(7 * h + k)
            wide = tile.shape[1]
            for t in range(2):
                for q in range(4):
                    send_a[t, 2 * q + h, :, k * 128 : k * 128 + wide] = tile[
                        t * 64 + q * 16 : t * 64 + q * 16 + 16
                    ]
    for c in a_out:
        c.start()

    total = send_g[xl, j].astype(F32)
    for n in range(15):
        g_out[n].wait_recv()
        total += recv_g[n].astype(F32)
    zsend[...] = total.astype(BF16)
    q_out = []
    for n, d in enumerate(Z_DELTAS):
        c = copy(zsend, zrecv.at[n], q_s.at[n], q_r.at[n], dev(dz=d))
        c.start()
        q_out.append(c)

    loads[2].wait()
    for p in range(2):
        patch = shifted[pl.ds(aligned((mine + p - 1) * ROWS, 64), KC), :]
        cells_tmp[p] = tn(patch, weight_t[...])
    for p in range(2):
        for zz in range(NZ):
            out_ref[p, :, zz * 128 : zz * 128 + 128] = cells_tmp[
                p, pl.ds(zz, NY, stride=NZ), :
            ].astype(BF16)

    cot_edge.wait_recv()

    @pl.when(s == 0)
    def _():
        cot_t[0] = jnp.zeros((COUT, CELLS), BF16)

    @pl.when(s == 31)
    def _():
        cot_t[5] = jnp.zeros((COUT, CELLS), BF16)

    w_cat = jnp.concatenate([weight_t[r * ROWS : (r + 1) * ROWS, :] for r in range(3)], axis=1)
    for p in range(2):
        here = 1 + 2 * core + p
        c_cat = jnp.concatenate([cot_t[here + 1], cot_t[here], cot_t[here - 1]], axis=0)
        spread = nn(w_cat, c_cat)
        back = jnp.zeros((CIN, CELLS), F32)
        for n in range(9):
            dy, dz = n // 3 - 1, n % 3 - 1
            part = spread[n * CIN : (n + 1) * CIN]
            turn = (dy * NZ + dz) % CELLS
            if turn:
                part = pltpu.roll(part, turn, 1)
            back += jnp.where(within(-dy, -dz), part, 0.0)
        cells_tmp[2 + p] = jnp.transpose(jnp.concatenate([back, back], axis=0))
    for p in range(2):
        for zp in range(NZ // 2):
            even = cells_tmp[2 + p, pl.ds(2 * zp, NY, stride=NZ), :]
            odd = cells_tmp[2 + p, pl.ds(2 * zp + 1, NY, stride=NZ), :]
            igrad_ref[p, :, zp * 128 : zp * 128 + 128] = jnp.where(lane[:NY] < 64, even, odd).astype(BF16)

    total = zsend[...].astype(F32)
    for n in range(7):
        q_out[n].wait_recv()
        total += zrecv[n].astype(F32)
    quarter = core * 2 + xl
    quarters[quarter] = total.astype(BF16)
    k_out = []
    for n, (device, other) in enumerate(
        ((xl_other, 3 - quarter), (xl_peer, core * 2 + 1 - xl), (dev(other=True), (1 - core) * 2 + xl))
    ):
        c = copy(quarters.at[quarter], quarters.at[quarter], k_s.at[n], k_r.at[n], device)
        c.start()
        k_out.append(c)
    loads[3].wait()
    ainv = ainv_ref[...]
    a_hi = ainv.astype(BF16)
    a_lo = (ainv - a_hi.astype(F32)).astype(BF16)

    piece = send_a[xl, j].astype(F32)
    for n in range(15):
        a_out[n].wait_recv()
        piece += recv_a[n].astype(F32)
    fin[j] = (piece * (1.0 / TOTAL)).astype(BF16)
    v_out = []
    for n, (dx, dy) in enumerate(SAMPLE_DELTAS):
        c = copy(fin.at[j], fin.at[j], v_s.at[n], v_r.at[n], dev(dx, dy))
        c.start()
        v_out.append(c)

    for c in k_out:
        c.wait_recv()
    grad = jnp.concatenate(
        [quarters[0], quarters[1, :, :384], quarters[2], quarters[3, :, :384]], axis=1
    )[:, :KC]
    half = (nt(grad, a_hi) + nt(grad, a_lo)) * (1.0 / TOTAL)
    hg[j, :, :128] = jnp.concatenate([half, jnp.zeros((16, 128 - SHARE), F32)], axis=1).astype(BF16)
    hg[j, :, 128:] = quarters[1, :, 384:]
    u_out = []
    for n, (dx, dy) in enumerate(SAMPLE_DELTAS):
        c = copy(hg.at[j], hg.at[j], u_s.at[n], u_r.at[n], dev(dx, dy))
        c.start()
        u_out.append(c)

    for c in v_out:
        c.wait_recv()
    fin_ref[...] = fin[...]
    for c in u_out:
        c.wait_recv()
    half_ref[...] = hg[...]

    for c in z_out + f_out + [cot_core, cot_edge, side_copy] + g_out + q_out + k_out + a_out + v_out + u_out:
        c.wait_send()

    @pl.when(edge_receiver)
    def _():
        edge_forward.wait_send()

    @pl.when(edge_sender)
    def _():
        for i in range(8):
            edge_copy(i).wait_send()


def finish_kernel(
    fin_ref, out_in, igrad_in, hg_ref, ginv_ref, out_ref, igrad_ref, a_ref, g_ref, update_ref
):
    out_ref[...] = out_in[...]
    igrad_ref[...] = igrad_in[...]
    for q in range(4):
        deep = min(16, SHARE - 16 * q)
        a_ref[16 * q : 16 * q + deep, :HALF] = fin_ref[2 * q][:deep].astype(F32)
        a_ref[16 * q : 16 * q + deep, HALF:] = fin_ref[2 * q + 1][:deep, : KC - HALF].astype(F32)
    hg = hg_ref[...].reshape(COUT, 256)
    g_ref[...] = hg[:, 128:].astype(F32) * (1.0 / TOTAL)
    update = lax.dot_general(
        ginv_ref[...], hg[:, :128].astype(F32), (((1,), (0,)), ((), ())),
        precision=lax.Precision.HIGHEST, preferred_element_type=F32,
    )
    update_ref[...] = jnp.transpose(update)[:SHARE]


def shards(activations, cotangent, weight, a_inverse, g_inverse):
    vmem = pl.BlockSpec(memory_space=pltpu.VMEM)
    dma = pltpu.SemaphoreType.DMA
    counts = (7, 7, 8, 8, 8, 1, 1, 1, 3, 3, 15, 15, 7, 7, 3, 3, 7, 7, 15, 15, 7, 7)
    fin, outs, igrad, hg = pl.pallas_call(
        step_kernel,
        out_shape=(
            pltpu.VMEM((8, 16, HALF), BF16),
            pltpu.VMEM((2, NY, NZ * COUT), BF16),
            pltpu.VMEM((2, NY, NZ * CIN), BF16),
            pltpu.VMEM((8, 16, 256), BF16),
        ),
        in_specs=[pl.BlockSpec(memory_space=pltpu.HBM)] * 4,
        out_specs=[vmem] * 4,
        scratch_shapes=[
            pltpu.VMEM((PLANES, CIN, CELLS), BF16),
            pltpu.VMEM(((PLANES + 1) * ROWS, CELLS), BF16),
            pltpu.VMEM((34, 128, CELLS), BF16),
            pltpu.VMEM((ROWS, 384), F32),
            pltpu.VMEM((CIN, CELLS), BF16),
            pltpu.VMEM((2, 80, CELLS), F32),
            pltpu.VMEM((4, CELLS, 128), F32),
            pltpu.VMEM((6, COUT, CELLS), BF16),
            pltpu.VMEM((2, NY, NZ * CIN), BF16),
            pltpu.VMEM((2, NY, NZ * COUT), BF16),
            pltpu.VMEM((KC, COUT), BF16),
            pltpu.VMEM((SHARE, KC), F32),
            dma((4,)),
            pltpu.VMEM((2, 8, 16, HALF), BF16),
            pltpu.VMEM((15, 16, HALF), BF16),
            pltpu.VMEM((8, 16, HALF), BF16),
            pltpu.VMEM((2, 8, 16, 512), BF16),
            pltpu.VMEM((15, 16, 512), BF16),
            pltpu.VMEM((16, 512), BF16),
            pltpu.VMEM((7, 16, 512), BF16),
            pltpu.VMEM((4, 16, 512), BF16),
            pltpu.VMEM((8, 16, 256), BF16),
        ]
        + [dma((n,)) for n in counts],
        compiler_params=pltpu.CompilerParams(
            collective_id=0, has_side_effects=True, vmem_limit_bytes=58 << 20
        ),
        cost_estimate=pl.CostEstimate(flops=2 * 10**9, bytes_accessed=2 * 10**6, transcendentals=0),
        name="step",
    )(activations[0], cotangent[0], weight.T, a_inverse)
    outputs, input_grad, a_factor, g_factor, update = pl.pallas_call(
        finish_kernel,
        out_shape=(
            jax.ShapeDtypeStruct((2, NY, NZ * COUT), BF16),
            jax.ShapeDtypeStruct((2, NY, NZ * CIN), BF16),
            jax.ShapeDtypeStruct((SHARE, KC), F32),
            jax.ShapeDtypeStruct((COUT, COUT), F32),
            jax.ShapeDtypeStruct((SHARE, COUT), F32),
        ),
        in_specs=[vmem] * 5,
        out_specs=[vmem] * 5,
        compiler_params=pltpu.CompilerParams(vmem_limit_bytes=16 << 20),
        name="finish",
    )(fin, outs, igrad, hg, g_inverse)
    return outputs[None], input_grad[None], a_factor, g_factor, update.T


def solution(mesh):
    return jax.shard_map(
        shards,
        mesh=mesh,
        in_specs=(
            P("sample", "space", None, None),
            P("sample", "space", None, None),
            P(),
            P("space", None),
            P(),
        ),
        out_specs=(
            P("sample", "space", None, None),
            P("sample", "space", None, None),
            P("space", None),
            P(),
            P(None, "space"),
        ),
        check_vma=False,
    )
```

```python
import jax
import jax.numpy as jnp
from jax import lax
from jax.experimental import pallas as pl
from jax.experimental.pallas import tpu as pltpu
from jax.sharding import PartitionSpec as P

MESH = pl.DeviceIdType.MESH
F32 = jnp.float32
BF16 = jnp.bfloat16

CIN, COUT = 64, 128
NY, NZ = 8, 16
CELLS = NY * NZ
KC = 27 * CIN
ROWS = 9 * CIN
SHARE = KC // 32
HALF = 896
PLANES = 34
TOTAL = float(8 * 64 * CELLS)

Z_DELTAS = (1, 7, 2, 6, 3, 5, 4)
XY_DELTAS = tuple(
    sorted(
        ((a, b) for a in range(4) for b in range(4) if (a, b) != (0, 0)),
        key=lambda d: -(min(d[0], 4 - d[0]) + min(d[1], 4 - d[1])),
    )
)
SAMPLE_DELTAS = tuple(d for d in XY_DELTAS if d[0] % 2 == 0)


def nt(left, right):
    return lax.dot_general(left, right, (((1,), (1,)), ((), ())), preferred_element_type=F32)


def nn(left, right):
    return lax.dot_general(left, right, (((1,), (0,)), ((), ())), preferred_element_type=F32)


def tn(left, right):
    return lax.dot_general(left, right, (((0,), (0,)), ((), ())), preferred_element_type=F32)


def aligned(value, unit):
    return pl.multiple_of(value, unit)


def step_kernel(
    act_hbm, cot_hbm, weight_hbm, ainv_hbm,
    fin_ref, out_ref, igrad_ref, half_ref,
    planes, shifted, chosen, acc, side, rows_tmp, cells_tmp, cot_t, act_ref, cot_ref, weight_t, ainv_ref, load,
    send_a, recv_a, fin, send_g, recv_g, zsend, zrecv, quarters, hg,
    z_s, z_r, f_s, f_r, b_s, b_r, bf_s, bf_r, c_s, c_r,
    g_s, g_r, q_s, q_r, k_s, k_r, u_s, u_r, a_s, a_r, v_s, v_r,
):
    j = lax.axis_index("sample")
    s = lax.axis_index("space")
    xh, y = j // 4, j % 4
    xl, z, core = s // 16, (s // 2) % 8, s % 2
    x = xh * 2 + xl

    def dev(dx=0, dy=0, dz=0, other=False):
        x2, y2, z2 = (x + dx) % 4, (y + dy) % 4, (z + dz) % 8
        c2 = 1 - core if other else core
        return {"sample": (x2 // 2) * 4 + y2, "space": ((x2 % 2) * 8 + z2) * 2 + c2}

    def at_space(s2):
        return {"sample": j, "space": s2}

    def copy(src, dst, ssem, rsem, device):
        return pltpu.make_async_remote_copy(
            src_ref=src, dst_ref=dst, send_sem=ssem, recv_sem=rsem,
            device_id=device, device_id_type=MESH,
        )

    across = at_space((s + 32 - 1 + 2 * core) % 32)
    xl_peer = at_space(((1 - xl) * 8 + z) * 2 + core)
    xl_other = at_space(((1 - xl) * 8 + z) * 2 + 1 - core)
    edge_sender = jnp.logical_and(z == 7 * (1 - xl), core == 1 - xl)
    edge_receiver = core == xl
    edge_slot = 33 * (1 - xl)
    edge_far = jnp.minimum((z + 1 - xl) % 8, (7 * (1 - xl) + 8 - z) % 8)
    edge_far = jnp.minimum(edge_far, 3)
    edge_soon = (edge_far + 1) // 2

    loads = [
        pltpu.make_async_copy(src, dst, load.at[n])
        for n, (src, dst) in enumerate(
            ((act_hbm, act_ref), (cot_hbm, cot_ref), (weight_hbm, weight_t), (ainv_hbm, ainv_ref))
        )
    ]
    for c in loads:
        c.start()

    barrier = pltpu.get_barrier_semaphore()

    def greet(device):
        pl.semaphore_signal(barrier, inc=1, device_id=device, device_id_type=MESH)

    for d in reversed(Z_DELTAS):
        greet(dev(dz=d))
    for dx, dy in XY_DELTAS:
        greet(dev(dx, dy))
    greet(dev(other=True))
    greet(xl_other)
    greet(across)

    @pl.when(edge_receiver)
    def _():
        greet(at_space(((1 - xl) * 8 + 7 * xl) * 2 + core))

    mine = 1 + 4 * z + 2 * core
    loads[0].wait()
    loads[1].wait()
    for p in range(2):
        for zz in range(NZ):
            pair = act_ref[p, :, (zz // 2) * 128 : (zz // 2) * 128 + 128].astype(F32)
            if zz % 2:
                pair = pltpu.roll(pair, 64, 1)
            cells_tmp[p, pl.ds(zz, NY, stride=NZ), :] = pair
    for p in range(2):
        for zz in range(NZ):
            cells_tmp[2 + p, pl.ds(zz, NY, stride=NZ), :] = cot_ref[
                p, :, zz * 128 : zz * 128 + 128
            ].astype(F32)
    for p in range(2):
        planes[mine + p] = jnp.transpose(cells_tmp[p])[:CIN].astype(BF16)
        cot_t[1 + 2 * core + p] = jnp.transpose(cells_tmp[2 + p]).astype(BF16)

    lane = lax.broadcasted_iota(jnp.int32, (CIN, CELLS), 1)
    ly, lz = lane // NZ, lane % NZ

    def within(dy, dz):
        return (ly + dy >= 0) & (ly + dy < NY) & (lz + dz >= 0) & (lz + dz < NZ)

    planes[33 * xl] = jnp.zeros((CIN, CELLS), BF16)

    def build_from(value, i):
        for n in range(9):
            dy, dz = n // 3 - 1, n % 3 - 1
            turn = -(dy * NZ + dz) % CELLS
            moved = pltpu.roll(value, turn, 1) if turn else value
            shifted[pl.ds(aligned(i * ROWS + n * CIN, 64), CIN), :] = jnp.where(
                within(dy, dz), moved, 0.0
            ).astype(BF16)

    def build(first, count):
        for q in range(count):
            build_from(planes[first + q].astype(F32), first + q)

    def put(first, count, ssem, rsem, device):
        ref = planes.at[pl.ds(first, count)]
        return copy(ref, ref, ssem, rsem, device)

    peers = len(Z_DELTAS) + len(XY_DELTAS) + 3
    pl.semaphore_wait(barrier, peers + jnp.where(edge_sender, 8, 0))

    cot_core = copy(
        cot_t.at[pl.ds(1 + 2 * core, 2)], cot_t.at[pl.ds(1 + 2 * core, 2)],
        c_s.at[0], c_r.at[0], dev(other=True),
    )
    cot_edge = copy(
        cot_t.at[1 + 3 * core], cot_t.at[5 * (1 - core)], c_s.at[1], c_r.at[1], across
    )
    side_copy = copy(planes.at[mine + core], side, c_s.at[2], c_r.at[2], across)
    z_out = []
    for n, d in enumerate(Z_DELTAS):
        z_out.append(put(mine, 2, z_s.at[n], z_r.at[n], dev(dz=d)))
    f_out = [put(mine, 2, f_s.at[0], f_r.at[0], dev(other=True))]

    def edge_copy(i):
        zz = (z + i) % 8
        return copy(
            planes.at[32 - 31 * xl], planes.at[33 * xl],
            b_s.at[i], b_r.at[0], at_space(((1 - xl) * 8 + zz) * 2 + core),
        )

    edge_order = (1, 0, 7, 2, 6, 3, 5, 4)
    z_out[0].start()
    z_out[1].start()
    side_copy.start()
    f_out[0].start()
    cot_core.start()

    @pl.when(edge_sender)
    def _():
        for i in edge_order:
            edge_copy(i).start()

    for c in z_out[2:]:
        c.start()
    cot_edge.start()

    edge_forward = put(edge_slot, 1, bf_s.at[0], bf_r.at[0], dev(other=True))

    def edge_arrive(level):
        @pl.when(jnp.logical_and(edge_receiver, edge_soon == level))
        def _():
            edge_copy(0).wait_recv()
            edge_forward.start()
            build(edge_slot, 1)

        @pl.when(jnp.logical_and(jnp.logical_not(edge_receiver), jnp.maximum(edge_far, 1) == level))
        def _():
            edge_forward.wait_recv()
            build(edge_slot, 1)

    def from_chip(n):
        return 1 + 4 * ((z + 8 - Z_DELTAS[n]) % 8)

    def arrive(n):
        z_out[n].wait_recv()
        c = put(from_chip(n) + 2 * core, 2, f_s.at[n + 1], f_r.at[n + 1], dev(other=True))
        c.start()
        f_out.append(c)

    build(33 * xl, 1)
    build(mine, 2)
    f_out[0].wait_recv()
    build(1 + 4 * z + 2 * (1 - core), 2)
    arrive(0)
    arrive(1)
    beside = 4 * z + 5 * (1 - core)

    @pl.when(jnp.logical_and(beside > 0, beside < 33))
    def _():
        build(beside, 1)

    side_copy.wait_recv()

    @pl.when(jnp.logical_and(s > 0, s < 31))
    def _():
        build_from(side[...].astype(F32), 4 * z + 5 * core)

    edge_arrive(0)

    cot_core.wait_recv()
    cot_cat = jnp.concatenate([cot_t[1], cot_t[2], cot_t[3], cot_t[4]], axis=1)

    def patch_cat(first, offset):
        return jnp.concatenate(
            [
                shifted[pl.ds(aligned((first + i - 1) * ROWS + offset, 64), HALF), :]
                for i in range(4)
            ],
            axis=1,
        )

    w_part = nt(cot_cat, patch_cat(4 * z + 1, core * HALF)).astype(BF16)
    g_part = nt(cot_cat, cot_cat).astype(BF16)
    for r in range(8):
        send_g[0, r] = w_part[r * 16 : r * 16 + 16, :512]
        send_g[1, r, :, :384] = w_part[r * 16 : r * 16 + 16, 512:]
        send_g[1, r, :, 384:] = g_part[r * 16 : r * 16 + 16]
    g_out = []
    for n, (dx, dy) in enumerate(XY_DELTAS):
        x2, y2 = (x + dx) % 4, (y + dy) % 4
        c = copy(
            send_g.at[x2 % 2, (x2 // 2) * 4 + y2], recv_g.at[n],
            g_s.at[n], g_r.at[n], dev(dx, dy),
        )
        c.start()
        g_out.append(c)

    first_row = SHARE * (2 * z + core)
    base = (first_row // 16) * 16
    off = first_row % 16

    def choose(i, carry):
        for t in range(2):
            start = aligned((i - 1) * ROWS + t * 16 * SHARE + base, 16)
            rows_tmp[t] = shifted[pl.ds(start, 80), :].astype(F32)
            chosen[i, t * 64 : t * 64 + 64, :] = rows_tmp[t, pl.ds(off, 64), :].astype(BF16)
        return carry

    chosen[0] = jnp.zeros((128, CELLS), BF16)
    chosen[33] = jnp.zeros((128, CELLS), BF16)

    def covariance(chips, fresh=False):
        for chip in chips:
            for i in range(6):
                choose(jnp.clip(4 * chip + i, 1, 32), 0)
        spots = [4 * chip + 1 + q for chip in chips for q in range(4)]
        left = jnp.concatenate(
            [shifted[pl.ds(aligned(i * ROWS, 64), ROWS), :] for i in spots], axis=1
        )
        right = jnp.concatenate(
            [jnp.concatenate([chosen[i - k] for i in spots], axis=1) for k in (-1, 0, 1)], axis=0
        )
        if fresh:
            acc[...] = nt(left, right)
        else:
            acc[...] += nt(left, right)

    toward = 1 - 2 * core

    def chip_at(d):
        return (z + 8 + d * toward) % 8

    def direct(*news):
        for n in news:
            arrive(n)
        for n in news:
            build(from_chip(n) + 2 * core, 2)

    def forwarded(*news):
        for n in news:
            f_out[n + 1].wait_recv()
        for n in news:
            build(from_chip(n) + 2 * (1 - core), 2)

    arrive(2)
    arrive(3)
    for n in range(4):
        build(from_chip(n) + 2 * core, 2)
    forwarded(0, 1)
    edge_arrive(1)
    covariance((z, chip_at(1)), fresh=True)
    direct(4, 5)
    forwarded(2, 3)
    edge_arrive(2)
    covariance((chip_at(-1), chip_at(2)))
    direct(6)
    forwarded(4, 5)
    edge_arrive(3)
    covariance((chip_at(-2), chip_at(3)))
    forwarded(6)
    covariance((chip_at(-3), chip_at(4)))

    @pl.when(xl == 0)
    def _():
        acc[:, 256:] += nt(shifted[33 * ROWS : 34 * ROWS, :], chosen[32])

    @pl.when(xl == 1)
    def _():
        acc[:, :128] += nt(shifted[:ROWS, :], chosen[1])

    def column_tile(k):
        parts = []
        start, stop = 128 * k, min(128 * k + 128, KC)
        while start < stop:
            kx, row = start // ROWS, start % ROWS
            deep = min(stop - start, ROWS - row)
            parts.append(acc[row : row + deep, kx * 128 : kx * 128 + 128])
            start += deep
        return jnp.transpose(jnp.concatenate(parts, axis=0)).astype(BF16)

    a_out = []
    for n, (dx, dy) in enumerate(XY_DELTAS):
        x2, y2 = (x + dx) % 4, (y + dy) % 4
        a_out.append(
            copy(
                send_a.at[x2 % 2, (x2 // 2) * 4 + y2], recv_a.at[n],
                a_s.at[n], a_r.at[n], dev(dx, dy),
            )
        )
    for h in range(2):
        for k in range(7):
            tile = column_tile(7 * h + k)
            wide = tile.shape[1]
            for t in range(2):
                for q in range(4):
                    send_a[t, 2 * q + h, :, k * 128 : k * 128 + wide] = tile[
                        t * 64 + q * 16 : t * 64 + q * 16 + 16
                    ]
    for c in a_out:
        c.start()

    total = send_g[xl, j].astype(F32)
    for n in range(15):
        g_out[n].wait_recv()
        total += recv_g[n].astype(F32)
    zsend[...] = total.astype(BF16)
    q_out = []
    for n, d in enumerate(Z_DELTAS):
        c = copy(zsend, zrecv.at[n], q_s.at[n], q_r.at[n], dev(dz=d))
        c.start()
        q_out.append(c)

    loads[2].wait()
    for p in range(2):
        patch = shifted[pl.ds(aligned((mine + p - 1) * ROWS, 64), KC), :]
        cells_tmp[p] = tn(patch, weight_t[...])
    for p in range(2):
        for zz in range(NZ):
            out_ref[p, :, zz * 128 : zz * 128 + 128] = cells_tmp[
                p, pl.ds(zz, NY, stride=NZ), :
            ].astype(BF16)

    cot_edge.wait_recv()

    @pl.when(s == 0)
    def _():
        cot_t[0] = jnp.zeros((COUT, CELLS), BF16)

    @pl.when(s == 31)
    def _():
        cot_t[5] = jnp.zeros((COUT, CELLS), BF16)

    w_cat = jnp.concatenate([weight_t[r * ROWS : (r + 1) * ROWS, :] for r in range(3)], axis=1)
    for p in range(2):
        here = 1 + 2 * core + p
        c_cat = jnp.concatenate([cot_t[here + 1], cot_t[here], cot_t[here - 1]], axis=0)
        spread = nn(w_cat, c_cat)
        back = jnp.zeros((CIN, CELLS), F32)
        for n in range(9):
            dy, dz = n // 3 - 1, n % 3 - 1
            part = spread[n * CIN : (n + 1) * CIN]
            turn = (dy * NZ + dz) % CELLS
            if turn:
                part = pltpu.roll(part, turn, 1)
            back += jnp.where(within(-dy, -dz), part, 0.0)
        cells_tmp[2 + p] = jnp.transpose(jnp.concatenate([back, back], axis=0))
    for p in range(2):
        for zp in range(NZ // 2):
            even = cells_tmp[2 + p, pl.ds(2 * zp, NY, stride=NZ), :]
            odd = cells_tmp[2 + p, pl.ds(2 * zp + 1, NY, stride=NZ), :]
            igrad_ref[p, :, zp * 128 : zp * 128 + 128] = jnp.where(lane[:NY] < 64, even, odd).astype(BF16)

    total = zsend[...].astype(F32)
    for n in range(7):
        q_out[n].wait_recv()
        total += zrecv[n].astype(F32)
    quarter = core * 2 + xl
    quarters[quarter] = total.astype(BF16)
    k_out = []
    for n, (device, other) in enumerate(
        ((xl_other, 3 - quarter), (xl_peer, core * 2 + 1 - xl), (dev(other=True), (1 - core) * 2 + xl))
    ):
        c = copy(quarters.at[quarter], quarters.at[quarter], k_s.at[n], k_r.at[n], device)
        c.start()
        k_out.append(c)
    loads[3].wait()
    ainv = ainv_ref[...]
    a_hi = ainv.astype(BF16)
    a_lo = (ainv - a_hi.astype(F32)).astype(BF16)

    piece = send_a[xl, j].astype(F32)
    for n in range(15):
        a_out[n].wait_recv()
        piece += recv_a[n].astype(F32)
    fin[j] = (piece * (1.0 / TOTAL)).astype(BF16)
    v_out = []
    for n, (dx, dy) in enumerate(SAMPLE_DELTAS):
        c = copy(fin.at[j], fin.at[j], v_s.at[n], v_r.at[n], dev(dx, dy))
        c.start()
        v_out.append(c)

    for c in k_out:
        c.wait_recv()
    grad = jnp.concatenate(
        [quarters[0], quarters[1, :, :384], quarters[2], quarters[3, :, :384]], axis=1
    )[:, :KC]
    half = (nt(grad, a_hi) + nt(grad, a_lo)) * (1.0 / TOTAL)
    hg[j, :, :128] = jnp.concatenate([half, jnp.zeros((16, 128 - SHARE), F32)], axis=1).astype(BF16)
    hg[j, :, 128:] = quarters[1, :, 384:]
    u_out = []
    for n, (dx, dy) in enumerate(SAMPLE_DELTAS):
        c = copy(hg.at[j], hg.at[j], u_s.at[n], u_r.at[n], dev(dx, dy))
        c.start()
        u_out.append(c)

    for c in v_out:
        c.wait_recv()
    fin_ref[...] = fin[...]
    for c in u_out:
        c.wait_recv()
    half_ref[...] = hg[...]

    for c in z_out + f_out + [cot_core, cot_edge, side_copy] + g_out + q_out + k_out + a_out + v_out + u_out:
        c.wait_send()

    @pl.when(edge_receiver)
    def _():
        edge_forward.wait_send()

    @pl.when(edge_sender)
    def _():
        for i in range(8):
            edge_copy(i).wait_send()


def finish_kernel(
    fin_ref, out_in, igrad_in, hg_ref, ginv_ref, out_ref, igrad_ref, a_ref, g_ref, update_ref
):
    out_ref[...] = out_in[...]
    igrad_ref[...] = igrad_in[...]
    for q in range(4):
        deep = min(16, SHARE - 16 * q)
        a_ref[16 * q : 16 * q + deep, :HALF] = fin_ref[2 * q][:deep].astype(F32)
        a_ref[16 * q : 16 * q + deep, HALF:] = fin_ref[2 * q + 1][:deep, : KC - HALF].astype(F32)
    hg = hg_ref[...].reshape(COUT, 256)
    g_ref[...] = hg[:, 128:].astype(F32) * (1.0 / TOTAL)
    update = lax.dot_general(
        ginv_ref[...], hg[:, :128].astype(F32), (((1,), (0,)), ((), ())),
        precision=lax.Precision.HIGHEST, preferred_element_type=F32,
    )
    update_ref[...] = jnp.transpose(update)[:SHARE]


def shards(activations, cotangent, weight, a_inverse, g_inverse):
    vmem = pl.BlockSpec(memory_space=pltpu.VMEM)
    dma = pltpu.SemaphoreType.DMA
    counts = (7, 7, 8, 8, 8, 1, 1, 1, 3, 3, 15, 15, 7, 7, 3, 3, 7, 7, 15, 15, 7, 7)
    fin, outs, igrad, hg = pl.pallas_call(
        step_kernel,
        out_shape=(
            pltpu.VMEM((8, 16, HALF), BF16),
            pltpu.VMEM((2, NY, NZ * COUT), BF16),
            pltpu.VMEM((2, NY, NZ * CIN), BF16),
            pltpu.VMEM((8, 16, 256), BF16),
        ),
        in_specs=[pl.BlockSpec(memory_space=pltpu.HBM)] * 4,
        out_specs=[vmem] * 4,
        scratch_shapes=[
            pltpu.VMEM((PLANES, CIN, CELLS), BF16),
            pltpu.VMEM(((PLANES + 1) * ROWS, CELLS), BF16),
            pltpu.VMEM((34, 128, CELLS), BF16),
            pltpu.VMEM((ROWS, 384), F32),
            pltpu.VMEM((CIN, CELLS), BF16),
            pltpu.VMEM((2, 80, CELLS), F32),
            pltpu.VMEM((4, CELLS, 128), F32),
            pltpu.VMEM((6, COUT, CELLS), BF16),
            pltpu.VMEM((2, NY, NZ * CIN), BF16),
            pltpu.VMEM((2, NY, NZ * COUT), BF16),
            pltpu.VMEM((KC, COUT), BF16),
            pltpu.VMEM((SHARE, KC), F32),
            dma((4,)),
            pltpu.VMEM((2, 8, 16, HALF), BF16),
            pltpu.VMEM((15, 16, HALF), BF16),
            pltpu.VMEM((8, 16, HALF), BF16),
            pltpu.VMEM((2, 8, 16, 512), BF16),
            pltpu.VMEM((15, 16, 512), BF16),
            pltpu.VMEM((16, 512), BF16),
            pltpu.VMEM((7, 16, 512), BF16),
            pltpu.VMEM((4, 16, 512), BF16),
            pltpu.VMEM((8, 16, 256), BF16),
        ]
        + [dma((n,)) for n in counts],
        compiler_params=pltpu.CompilerParams(
            collective_id=0, has_side_effects=True, vmem_limit_bytes=58 << 20
        ),
        cost_estimate=pl.CostEstimate(flops=2 * 10**9, bytes_accessed=2 * 10**6, transcendentals=0),
        name="step",
    )(activations[0], cotangent[0], weight.T, a_inverse)
    outputs, input_grad, a_factor, g_factor, update = pl.pallas_call(
        finish_kernel,
        out_shape=(
            jax.ShapeDtypeStruct((2, NY, NZ * COUT), BF16),
            jax.ShapeDtypeStruct((2, NY, NZ * CIN), BF16),
            jax.ShapeDtypeStruct((SHARE, KC), F32),
            jax.ShapeDtypeStruct((COUT, COUT), F32),
            jax.ShapeDtypeStruct((SHARE, COUT), F32),
        ),
        in_specs=[vmem] * 5,
        out_specs=[vmem] * 5,
        compiler_params=pltpu.CompilerParams(vmem_limit_bytes=16 << 20),
        name="finish",
    )(fin, outs, igrad, hg, g_inverse)
    return outputs[None], input_grad[None], a_factor, g_factor, update.T


def solution(mesh):
    return jax.shard_map(
        shards,
        mesh=mesh,
        in_specs=(
            P("sample", "space", None, None),
            P("sample", "space", None, None),
            P(),
            P("space", None),
            P(),
        ),
        out_specs=(
            P("sample", "space", None, None),
            P("sample", "space", None, None),
            P("space", None),
            P(),
            P(None, "space"),
        ),
        check_vma=False,
    )
```

```python
import jax
import jax.numpy as jnp
from jax import lax
from jax.experimental import pallas as pl
from jax.experimental.pallas import tpu as pltpu
from jax.sharding import PartitionSpec as P

MESH = pl.DeviceIdType.MESH
F32 = jnp.float32
BF16 = jnp.bfloat16

CIN, COUT = 64, 128
NY, NZ = 8, 16
CELLS = NY * NZ
KC = 27 * CIN
ROWS = 9 * CIN
SHARE = KC // 32
HALF = 896
PLANES = 34
TOTAL = float(8 * 64 * CELLS)

Z_DELTAS = (1, 7, 2, 6, 3, 5, 4)
XY_DELTAS = tuple(
    sorted(
        ((a, b) for a in range(4) for b in range(4) if (a, b) != (0, 0)),
        key=lambda d: -(min(d[0], 4 - d[0]) + min(d[1], 4 - d[1])),
    )
)
SAMPLE_DELTAS = tuple(d for d in XY_DELTAS if d[0] % 2 == 0)


def nt(left, right):
    return lax.dot_general(left, right, (((1,), (1,)), ((), ())), preferred_element_type=F32)


def nn(left, right):
    return lax.dot_general(left, right, (((1,), (0,)), ((), ())), preferred_element_type=F32)


def tn(left, right):
    return lax.dot_general(left, right, (((0,), (0,)), ((), ())), preferred_element_type=F32)


def aligned(value, unit):
    return pl.multiple_of(value, unit)


def step_kernel(
    act_hbm, cot_hbm, weight_hbm, ainv_hbm,
    fin_ref, out_ref, igrad_ref, half_ref,
    planes, shifted, chosen, acc, side, rows_tmp, cells_tmp, cot_t, act_ref, cot_ref, weight_t, ainv_ref, load,
    send_a, recv_a, fin, send_g, recv_g, zsend, zrecv, quarters, hg,
    z_s, z_r, f_s, f_r, b_s, b_r, bf_s, bf_r, c_s, c_r,
    g_s, g_r, q_s, q_r, k_s, k_r, u_s, u_r, a_s, a_r, v_s, v_r,
):
    j = lax.axis_index("sample")
    s = lax.axis_index("space")
    xh, y = j // 4, j % 4
    xl, z, core = s // 16, (s // 2) % 8, s % 2
    x = xh * 2 + xl

    def dev(dx=0, dy=0, dz=0, other=False):
        x2, y2, z2 = (x + dx) % 4, (y + dy) % 4, (z + dz) % 8
        c2 = 1 - core if other else core
        return {"sample": (x2 // 2) * 4 + y2, "space": ((x2 % 2) * 8 + z2) * 2 + c2}

    def at_space(s2):
        return {"sample": j, "space": s2}

    def copy(src, dst, ssem, rsem, device):
        return pltpu.make_async_remote_copy(
            src_ref=src, dst_ref=dst, send_sem=ssem, recv_sem=rsem,
            device_id=device, device_id_type=MESH,
        )

    across = at_space((s + 32 - 1 + 2 * core) % 32)
    xl_peer = at_space(((1 - xl) * 8 + z) * 2 + core)
    xl_other = at_space(((1 - xl) * 8 + z) * 2 + 1 - core)
    edge_sender = jnp.logical_and(z == 7 * (1 - xl), core == 1 - xl)
    edge_receiver = core == xl
    edge_slot = 33 * (1 - xl)
    edge_far = jnp.minimum((z + 1 - xl) % 8, (7 * (1 - xl) + 8 - z) % 8)
    edge_far = jnp.minimum(edge_far, 3)
    edge_soon = (edge_far + 1) // 2

    loads = [
        pltpu.make_async_copy(src, dst, load.at[n])
        for n, (src, dst) in enumerate(
            ((act_hbm, act_ref), (cot_hbm, cot_ref), (weight_hbm, weight_t), (ainv_hbm, ainv_ref))
        )
    ]
    for c in loads:
        c.start()

    barrier = pltpu.get_barrier_semaphore()

    def greet(device):
        pl.semaphore_signal(barrier, inc=1, device_id=device, device_id_type=MESH)

    for d in reversed(Z_DELTAS):
        greet(dev(dz=d))
    for dx, dy in XY_DELTAS:
        greet(dev(dx, dy))
    greet(dev(other=True))
    greet(xl_other)
    greet(across)

    @pl.when(edge_receiver)
    def _():
        greet(at_space(((1 - xl) * 8 + 7 * xl) * 2 + core))

    mine = 1 + 4 * z + 2 * core
    loads[0].wait()
    loads[1].wait()
    for p in range(2):
        for zz in range(NZ):
            pair = act_ref[p, :, (zz // 2) * 128 : (zz // 2) * 128 + 128].astype(F32)
            if zz % 2:
                pair = pltpu.roll(pair, 64, 1)
            cells_tmp[p, pl.ds(zz, NY, stride=NZ), :] = pair
    for p in range(2):
        for zz in range(NZ):
            cells_tmp[2 + p, pl.ds(zz, NY, stride=NZ), :] = cot_ref[
                p, :, zz * 128 : zz * 128 + 128
            ].astype(F32)
    for p in range(2):
        planes[mine + p] = jnp.transpose(cells_tmp[p])[:CIN].astype(BF16)
        cot_t[1 + 2 * core + p] = jnp.transpose(cells_tmp[2 + p]).astype(BF16)

    lane = lax.broadcasted_iota(jnp.int32, (CIN, CELLS), 1)
    ly, lz = lane // NZ, lane % NZ

    def within(dy, dz):
        return (ly + dy >= 0) & (ly + dy < NY) & (lz + dz >= 0) & (lz + dz < NZ)

    planes[33 * xl] = jnp.zeros((CIN, CELLS), BF16)

    def build_from(value, i):
        for n in range(9):
            dy, dz = n // 3 - 1, n % 3 - 1
            turn = -(dy * NZ + dz) % CELLS
            moved = pltpu.roll(value, turn, 1) if turn else value
            shifted[pl.ds(aligned(i * ROWS + n * CIN, 64), CIN), :] = jnp.where(
                within(dy, dz), moved, 0.0
            ).astype(BF16)

    def build(first, count):
        for q in range(count):
            build_from(planes[first + q].astype(F32), first + q)

    def put(first, count, ssem, rsem, device):
        ref = planes.at[pl.ds(first, count)]
        return copy(ref, ref, ssem, rsem, device)

    peers = len(Z_DELTAS) + len(XY_DELTAS) + 3
    pl.semaphore_wait(barrier, peers + jnp.where(edge_sender, 8, 0))

    cot_core = copy(
        cot_t.at[pl.ds(1 + 2 * core, 2)], cot_t.at[pl.ds(1 + 2 * core, 2)],
        c_s.at[0], c_r.at[0], dev(other=True),
    )
    cot_edge = copy(
        cot_t.at[1 + 3 * core], cot_t.at[5 * (1 - core)], c_s.at[1], c_r.at[1], across
    )
    side_copy = copy(planes.at[mine + core], side, c_s.at[2], c_r.at[2], across)
    z_out = []
    for n, d in enumerate(Z_DELTAS):
        z_out.append(put(mine, 2, z_s.at[n], z_r.at[n], dev(dz=d)))
    f_out = [put(mine, 2, f_s.at[0], f_r.at[0], dev(other=True))]

    def edge_copy(i):
        zz = (z + i) % 8
        return copy(
            planes.at[32 - 31 * xl], planes.at[33 * xl],
            b_s.at[i], b_r.at[0], at_space(((1 - xl) * 8 + zz) * 2 + core),
        )

    edge_order = (1, 0, 7, 2, 6, 3, 5, 4)
    z_out[0].start()
    z_out[1].start()
    side_copy.start()
    f_out[0].start()
    cot_core.start()

    @pl.when(edge_sender)
    def _():
        for i in edge_order:
            edge_copy(i).start()

    for c in z_out[2:]:
        c.start()
    cot_edge.start()

    edge_forward = put(edge_slot, 1, bf_s.at[0], bf_r.at[0], dev(other=True))

    def edge_arrive(level):
        @pl.when(jnp.logical_and(edge_receiver, edge_soon == level))
        def _():
            edge_copy(0).wait_recv()
            edge_forward.start()
            build(edge_slot, 1)

        @pl.when(jnp.logical_and(jnp.logical_not(edge_receiver), jnp.maximum(edge_far, 1) == level))
        def _():
            edge_forward.wait_recv()
            build(edge_slot, 1)

    def from_chip(n):
        return 1 + 4 * ((z + 8 - Z_DELTAS[n]) % 8)

    def arrive(n):
        z_out[n].wait_recv()
        c = put(from_chip(n) + 2 * core, 2, f_s.at[n + 1], f_r.at[n + 1], dev(other=True))
        c.start()
        f_out.append(c)

    build(33 * xl, 1)
    build(mine, 2)
    f_out[0].wait_recv()
    build(1 + 4 * z + 2 * (1 - core), 2)
    arrive(0)
    arrive(1)
    beside = 4 * z + 5 * (1 - core)

    @pl.when(jnp.logical_and(beside > 0, beside < 33))
    def _():
        build(beside, 1)

    side_copy.wait_recv()

    @pl.when(jnp.logical_and(s > 0, s < 31))
    def _():
        build_from(side[...].astype(F32), 4 * z + 5 * core)

    edge_arrive(0)

    cot_core.wait_recv()
    cot_cat = jnp.concatenate([cot_t[1], cot_t[2], cot_t[3], cot_t[4]], axis=1)

    def patch_cat(first, offset):
        return jnp.concatenate(
            [
                shifted[pl.ds(aligned((first + i - 1) * ROWS + offset, 64), HALF), :]
                for i in range(4)
            ],
            axis=1,
        )

    w_part = nt(cot_cat, patch_cat(4 * z + 1, core * HALF)).astype(BF16)
    g_part = nt(cot_cat, cot_cat).astype(BF16)
    for r in range(8):
        send_g[0, r] = w_part[r * 16 : r * 16 + 16, :512]
        send_g[1, r, :, :384] = w_part[r * 16 : r * 16 + 16, 512:]
        send_g[1, r, :, 384:] = g_part[r * 16 : r * 16 + 16]
    g_out = []
    for n, (dx, dy) in enumerate(XY_DELTAS):
        x2, y2 = (x + dx) % 4, (y + dy) % 4
        c = copy(
            send_g.at[x2 % 2, (x2 // 2) * 4 + y2], recv_g.at[n],
            g_s.at[n], g_r.at[n], dev(dx, dy),
        )
        c.start()
        g_out.append(c)

    first_row = SHARE * (2 * z + core)
    base = (first_row // 16) * 16
    off = first_row % 16

    def choose(i, carry):
        for t in range(2):
            start = aligned((i - 1) * ROWS + t * 16 * SHARE + base, 16)
            rows_tmp[t] = shifted[pl.ds(start, 80), :].astype(F32)
            chosen[i, t * 64 : t * 64 + 64, :] = rows_tmp[t, pl.ds(off, 64), :].astype(BF16)
        return carry

    chosen[0] = jnp.zeros((128, CELLS), BF16)
    chosen[33] = jnp.zeros((128, CELLS), BF16)

    def covariance(chips, fresh=False):
        for chip in chips:
            for i in range(6):
                choose(jnp.clip(4 * chip + i, 1, 32), 0)
        spots = [4 * chip + 1 + q for chip in chips for q in range(4)]
        left = jnp.concatenate(
            [shifted[pl.ds(aligned(i * ROWS, 64), ROWS), :] for i in spots], axis=1
        )
        right = jnp.concatenate(
            [jnp.concatenate([chosen[i - k] for i in spots], axis=1) for k in (-1, 0, 1)], axis=0
        )
        if fresh:
            acc[...] = nt(left, right)
        else:
            acc[...] += nt(left, right)

    toward = 1 - 2 * core

    def chip_at(d):
        return (z + 8 + d * toward) % 8

    def direct(*news):
        for n in news:
            arrive(n)
        for n in news:
            build(from_chip(n) + 2 * core, 2)

    def forwarded(*news):
        for n in news:
            f_out[n + 1].wait_recv()
        for n in news:
            build(from_chip(n) + 2 * (1 - core), 2)

    arrive(2)
    arrive(3)
    for n in range(4):
        build(from_chip(n) + 2 * core, 2)
    forwarded(0, 1)
    edge_arrive(1)
    covariance((z, chip_at(1)), fresh=True)
    direct(4, 5)
    forwarded(2, 3)
    edge_arrive(2)
    covariance((chip_at(-1), chip_at(2)))
    direct(6)
    forwarded(4, 5)
    total = send_g[xl, j].astype(F32)
    for n in range(15):
        g_out[n].wait_recv()
        total += recv_g[n].astype(F32)
    zsend[...] = total.astype(BF16)
    q_out = []
    for n, d in enumerate(Z_DELTAS):
        c = copy(zsend, zrecv.at[n], q_s.at[n], q_r.at[n], dev(dz=d))
        c.start()
        q_out.append(c)

    edge_arrive(3)
    covariance((chip_at(-2), chip_at(3)))
    forwarded(6)
    covariance((chip_at(-3), chip_at(4)))

    @pl.when(xl == 0)
    def _():
        acc[:, 256:] += nt(shifted[33 * ROWS : 34 * ROWS, :], chosen[32])

    @pl.when(xl == 1)
    def _():
        acc[:, :128] += nt(shifted[:ROWS, :], chosen[1])

    def column_tile(k):
        parts = []
        start, stop = 128 * k, min(128 * k + 128, KC)
        while start < stop:
            kx, row = start // ROWS, start % ROWS
            deep = min(stop - start, ROWS - row)
            parts.append(acc[row : row + deep, kx * 128 : kx * 128 + 128])
            start += deep
        return jnp.transpose(jnp.concatenate(parts, axis=0)).astype(BF16)

    a_out = []
    for n, (dx, dy) in enumerate(XY_DELTAS):
        x2, y2 = (x + dx) % 4, (y + dy) % 4
        a_out.append(
            copy(
                send_a.at[x2 % 2, (x2 // 2) * 4 + y2], recv_a.at[n],
                a_s.at[n], a_r.at[n], dev(dx, dy),
            )
        )
    for h in range(2):
        for k in range(7):
            tile = column_tile(7 * h + k)
            wide = tile.shape[1]
            for t in range(2):
                for q in range(4):
                    send_a[t, 2 * q + h, :, k * 128 : k * 128 + wide] = tile[
                        t * 64 + q * 16 : t * 64 + q * 16 + 16
                    ]
    for c in a_out:
        c.start()

    loads[2].wait()
    for p in range(2):
        patch = shifted[pl.ds(aligned((mine + p - 1) * ROWS, 64), KC), :]
        cells_tmp[p] = tn(patch, weight_t[...])
    for p in range(2):
        for zz in range(NZ):
            out_ref[p, :, zz * 128 : zz * 128 + 128] = cells_tmp[
                p, pl.ds(zz, NY, stride=NZ), :
            ].astype(BF16)

    cot_edge.wait_recv()

    @pl.when(s == 0)
    def _():
        cot_t[0] = jnp.zeros((COUT, CELLS), BF16)

    @pl.when(s == 31)
    def _():
        cot_t[5] = jnp.zeros((COUT, CELLS), BF16)

    w_cat = jnp.concatenate([weight_t[r * ROWS : (r + 1) * ROWS, :] for r in range(3)], axis=1)
    for p in range(2):
        here = 1 + 2 * core + p
        c_cat = jnp.concatenate([cot_t[here + 1], cot_t[here], cot_t[here - 1]], axis=0)
        spread = nn(w_cat, c_cat)
        back = jnp.zeros((CIN, CELLS), F32)
        for n in range(9):
            dy, dz = n // 3 - 1, n % 3 - 1
            part = spread[n * CIN : (n + 1) * CIN]
            turn = (dy * NZ + dz) % CELLS
            if turn:
                part = pltpu.roll(part, turn, 1)
            back += jnp.where(within(-dy, -dz), part, 0.0)
        cells_tmp[2 + p] = jnp.transpose(jnp.concatenate([back, back], axis=0))
    for p in range(2):
        for zp in range(NZ // 2):
            even = cells_tmp[2 + p, pl.ds(2 * zp, NY, stride=NZ), :]
            odd = cells_tmp[2 + p, pl.ds(2 * zp + 1, NY, stride=NZ), :]
            igrad_ref[p, :, zp * 128 : zp * 128 + 128] = jnp.where(lane[:NY] < 64, even, odd).astype(BF16)

    total = zsend[...].astype(F32)
    for n in range(7):
        q_out[n].wait_recv()
        total += zrecv[n].astype(F32)
    quarter = core * 2 + xl
    quarters[quarter] = total.astype(BF16)
    k_out = []
    for n, (device, other) in enumerate(
        ((xl_other, 3 - quarter), (xl_peer, core * 2 + 1 - xl), (dev(other=True), (1 - core) * 2 + xl))
    ):
        c = copy(quarters.at[quarter], quarters.at[quarter], k_s.at[n], k_r.at[n], device)
        c.start()
        k_out.append(c)
    loads[3].wait()
    ainv = ainv_ref[...]
    a_hi = ainv.astype(BF16)
    a_lo = (ainv - a_hi.astype(F32)).astype(BF16)

    piece = send_a[xl, j].astype(F32)
    for n in range(15):
        a_out[n].wait_recv()
        piece += recv_a[n].astype(F32)
    fin[j] = (piece * (1.0 / TOTAL)).astype(BF16)
    v_out = []
    for n, (dx, dy) in enumerate(SAMPLE_DELTAS):
        c = copy(fin.at[j], fin.at[j], v_s.at[n], v_r.at[n], dev(dx, dy))
        c.start()
        v_out.append(c)

    for c in k_out:
        c.wait_recv()
    grad = jnp.concatenate(
        [quarters[0], quarters[1, :, :384], quarters[2], quarters[3, :, :384]], axis=1
    )[:, :KC]
    half = (nt(grad, a_hi) + nt(grad, a_lo)) * (1.0 / TOTAL)
    hg[j, :, :128] = jnp.concatenate([half, jnp.zeros((16, 128 - SHARE), F32)], axis=1).astype(BF16)
    hg[j, :, 128:] = quarters[1, :, 384:]
    u_out = []
    for n, (dx, dy) in enumerate(SAMPLE_DELTAS):
        c = copy(hg.at[j], hg.at[j], u_s.at[n], u_r.at[n], dev(dx, dy))
        c.start()
        u_out.append(c)

    for c in v_out:
        c.wait_recv()
    fin_ref[...] = fin[...]
    for c in u_out:
        c.wait_recv()
    half_ref[...] = hg[...]

    for c in z_out + f_out + [cot_core, cot_edge, side_copy] + g_out + q_out + k_out + a_out + v_out + u_out:
        c.wait_send()

    @pl.when(edge_receiver)
    def _():
        edge_forward.wait_send()

    @pl.when(edge_sender)
    def _():
        for i in range(8):
            edge_copy(i).wait_send()


def finish_kernel(
    fin_ref, out_in, igrad_in, hg_ref, ginv_ref, out_ref, igrad_ref, a_ref, g_ref, update_ref
):
    out_ref[...] = out_in[...]
    igrad_ref[...] = igrad_in[...]
    for q in range(4):
        deep = min(16, SHARE - 16 * q)
        a_ref[16 * q : 16 * q + deep, :HALF] = fin_ref[2 * q][:deep].astype(F32)
        a_ref[16 * q : 16 * q + deep, HALF:] = fin_ref[2 * q + 1][:deep, : KC - HALF].astype(F32)
    hg = hg_ref[...].reshape(COUT, 256)
    g_ref[...] = hg[:, 128:].astype(F32) * (1.0 / TOTAL)
    update = lax.dot_general(
        ginv_ref[...], hg[:, :128].astype(F32), (((1,), (0,)), ((), ())),
        precision=lax.Precision.HIGHEST, preferred_element_type=F32,
    )
    update_ref[...] = jnp.transpose(update)[:SHARE]


def shards(activations, cotangent, weight, a_inverse, g_inverse):
    vmem = pl.BlockSpec(memory_space=pltpu.VMEM)
    dma = pltpu.SemaphoreType.DMA
    counts = (7, 7, 8, 8, 8, 1, 1, 1, 3, 3, 15, 15, 7, 7, 3, 3, 7, 7, 15, 15, 7, 7)
    fin, outs, igrad, hg = pl.pallas_call(
        step_kernel,
        out_shape=(
            pltpu.VMEM((8, 16, HALF), BF16),
            pltpu.VMEM((2, NY, NZ * COUT), BF16),
            pltpu.VMEM((2, NY, NZ * CIN), BF16),
            pltpu.VMEM((8, 16, 256), BF16),
        ),
        in_specs=[pl.BlockSpec(memory_space=pltpu.HBM)] * 4,
        out_specs=[vmem] * 4,
        scratch_shapes=[
            pltpu.VMEM((PLANES, CIN, CELLS), BF16),
            pltpu.VMEM(((PLANES + 1) * ROWS, CELLS), BF16),
            pltpu.VMEM((34, 128, CELLS), BF16),
            pltpu.VMEM((ROWS, 384), F32),
            pltpu.VMEM((CIN, CELLS), BF16),
            pltpu.VMEM((2, 80, CELLS), F32),
            pltpu.VMEM((4, CELLS, 128), F32),
            pltpu.VMEM((6, COUT, CELLS), BF16),
            pltpu.VMEM((2, NY, NZ * CIN), BF16),
            pltpu.VMEM((2, NY, NZ * COUT), BF16),
            pltpu.VMEM((KC, COUT), BF16),
            pltpu.VMEM((SHARE, KC), F32),
            dma((4,)),
            pltpu.VMEM((2, 8, 16, HALF), BF16),
            pltpu.VMEM((15, 16, HALF), BF16),
            pltpu.VMEM((8, 16, HALF), BF16),
            pltpu.VMEM((2, 8, 16, 512), BF16),
            pltpu.VMEM((15, 16, 512), BF16),
            pltpu.VMEM((16, 512), BF16),
            pltpu.VMEM((7, 16, 512), BF16),
            pltpu.VMEM((4, 16, 512), BF16),
            pltpu.VMEM((8, 16, 256), BF16),
        ]
        + [dma((n,)) for n in counts],
        compiler_params=pltpu.CompilerParams(
            collective_id=0, has_side_effects=True, vmem_limit_bytes=58 << 20
        ),
        cost_estimate=pl.CostEstimate(flops=2 * 10**9, bytes_accessed=2 * 10**6, transcendentals=0),
        name="step",
    )(activations[0], cotangent[0], weight.T, a_inverse)
    outputs, input_grad, a_factor, g_factor, update = pl.pallas_call(
        finish_kernel,
        out_shape=(
            jax.ShapeDtypeStruct((2, NY, NZ * COUT), BF16),
            jax.ShapeDtypeStruct((2, NY, NZ * CIN), BF16),
            jax.ShapeDtypeStruct((SHARE, KC), F32),
            jax.ShapeDtypeStruct((COUT, COUT), F32),
            jax.ShapeDtypeStruct((SHARE, COUT), F32),
        ),
        in_specs=[vmem] * 5,
        out_specs=[vmem] * 5,
        compiler_params=pltpu.CompilerParams(vmem_limit_bytes=16 << 20),
        name="finish",
    )(fin, outs, igrad, hg, g_inverse)
    return outputs[None], input_grad[None], a_factor, g_factor, update.T


def solution(mesh):
    return jax.shard_map(
        shards,
        mesh=mesh,
        in_specs=(
            P("sample", "space", None, None),
            P("sample", "space", None, None),
            P(),
            P("space", None),
            P(),
        ),
        out_specs=(
            P("sample", "space", None, None),
            P("sample", "space", None, None),
            P("space", None),
            P(),
            P(None, "space"),
        ),
        check_vma=False,
    )
```

```python
import jax
import jax.numpy as jnp
from jax import lax
from jax.experimental import pallas as pl
from jax.experimental.pallas import tpu as pltpu
from jax.sharding import PartitionSpec as P

MESH = pl.DeviceIdType.MESH
F32 = jnp.float32
BF16 = jnp.bfloat16

CIN, COUT = 64, 128
NY, NZ = 8, 16
CELLS = NY * NZ
KC = 27 * CIN
ROWS = 9 * CIN
SHARE = KC // 32
HALF = 896
PLANES = 34
TOTAL = float(8 * 64 * CELLS)

Z_DELTAS = (1, 7, 2, 6, 3, 5, 4)
XY_DELTAS = tuple(
    sorted(
        ((a, b) for a in range(4) for b in range(4) if (a, b) != (0, 0)),
        key=lambda d: -(min(d[0], 4 - d[0]) + min(d[1], 4 - d[1])),
    )
)
SAMPLE_DELTAS = tuple(d for d in XY_DELTAS if d[0] % 2 == 0)


def nt(left, right):
    return lax.dot_general(left, right, (((1,), (1,)), ((), ())), preferred_element_type=F32)


def nn(left, right):
    return lax.dot_general(left, right, (((1,), (0,)), ((), ())), preferred_element_type=F32)


def tn(left, right):
    return lax.dot_general(left, right, (((0,), (0,)), ((), ())), preferred_element_type=F32)


def aligned(value, unit):
    return pl.multiple_of(value, unit)


def step_kernel(
    act_hbm, cot_hbm, weight_hbm, ainv_hbm,
    fin, out_ref, igrad_ref, hg,
    planes, shifted, chosen, acc, side, rows_tmp, cells_tmp, cot_t, act_ref, cot_ref, weight_t, ainv_ref, load,
    send_a, recv_a, send_g, recv_g, zsend, zrecv, quarters,
    z_s, z_r, f_s, f_r, b_s, b_r, bf_s, bf_r, c_s, c_r,
    g_s, g_r, q_s, q_r, k_s, k_r, u_s, u_r, a_s, a_r, v_s, v_r,
):
    j = lax.axis_index("sample")
    s = lax.axis_index("space")
    xh, y = j // 4, j % 4
    xl, z, core = s // 16, (s // 2) % 8, s % 2
    x = xh * 2 + xl

    def dev(dx=0, dy=0, dz=0, other=False):
        x2, y2, z2 = (x + dx) % 4, (y + dy) % 4, (z + dz) % 8
        c2 = 1 - core if other else core
        return {"sample": (x2 // 2) * 4 + y2, "space": ((x2 % 2) * 8 + z2) * 2 + c2}

    def at_space(s2):
        return {"sample": j, "space": s2}

    def copy(src, dst, ssem, rsem, device):
        return pltpu.make_async_remote_copy(
            src_ref=src, dst_ref=dst, send_sem=ssem, recv_sem=rsem,
            device_id=device, device_id_type=MESH,
        )

    across = at_space((s + 32 - 1 + 2 * core) % 32)
    xl_peer = at_space(((1 - xl) * 8 + z) * 2 + core)
    xl_other = at_space(((1 - xl) * 8 + z) * 2 + 1 - core)
    edge_sender = jnp.logical_and(z == 7 * (1 - xl), core == 1 - xl)
    edge_receiver = core == xl
    edge_slot = 33 * (1 - xl)
    edge_far = jnp.minimum((z + 1 - xl) % 8, (7 * (1 - xl) + 8 - z) % 8)
    edge_far = jnp.minimum(edge_far, 3)
    edge_soon = (edge_far + 1) // 2

    loads = [
        pltpu.make_async_copy(src, dst, load.at[n])
        for n, (src, dst) in enumerate(
            ((act_hbm, act_ref), (cot_hbm, cot_ref), (weight_hbm, weight_t), (ainv_hbm, ainv_ref))
        )
    ]
    for c in loads:
        c.start()

    barrier = pltpu.get_barrier_semaphore()

    def greet(device):
        pl.semaphore_signal(barrier, inc=1, device_id=device, device_id_type=MESH)

    for d in reversed(Z_DELTAS):
        greet(dev(dz=d))
    for dx, dy in XY_DELTAS:
        greet(dev(dx, dy))
    greet(dev(other=True))
    greet(xl_other)
    greet(across)

    @pl.when(edge_receiver)
    def _():
        greet(at_space(((1 - xl) * 8 + 7 * xl) * 2 + core))

    mine = 1 + 4 * z + 2 * core
    loads[0].wait()
    loads[1].wait()
    for p in range(2):
        for zz in range(NZ):
            pair = act_ref[p, :, (zz // 2) * 128 : (zz // 2) * 128 + 128].astype(F32)
            if zz % 2:
                pair = pltpu.roll(pair, 64, 1)
            cells_tmp[p, pl.ds(zz, NY, stride=NZ), :] = pair
    for p in range(2):
        for zz in range(NZ):
            cells_tmp[2 + p, pl.ds(zz, NY, stride=NZ), :] = cot_ref[
                p, :, zz * 128 : zz * 128 + 128
            ].astype(F32)
    for p in range(2):
        planes[mine + p] = jnp.transpose(cells_tmp[p])[:CIN].astype(BF16)
        cot_t[1 + 2 * core + p] = jnp.transpose(cells_tmp[2 + p]).astype(BF16)

    lane = lax.broadcasted_iota(jnp.int32, (CIN, CELLS), 1)
    ly, lz = lane // NZ, lane % NZ

    def within(dy, dz):
        return (ly + dy >= 0) & (ly + dy < NY) & (lz + dz >= 0) & (lz + dz < NZ)

    planes[33 * xl] = jnp.zeros((CIN, CELLS), BF16)

    def build_from(value, i):
        for n in range(9):
            dy, dz = n // 3 - 1, n % 3 - 1
            turn = -(dy * NZ + dz) % CELLS
            moved = pltpu.roll(value, turn, 1) if turn else value
            shifted[pl.ds(aligned(i * ROWS + n * CIN, 64), CIN), :] = jnp.where(
                within(dy, dz), moved, 0.0
            ).astype(BF16)

    def build(first, count):
        for q in range(count):
            build_from(planes[first + q].astype(F32), first + q)

    def put(first, count, ssem, rsem, device):
        ref = planes.at[pl.ds(first, count)]
        return copy(ref, ref, ssem, rsem, device)

    peers = len(Z_DELTAS) + len(XY_DELTAS) + 3
    pl.semaphore_wait(barrier, peers + jnp.where(edge_sender, 8, 0))

    cot_core = copy(
        cot_t.at[pl.ds(1 + 2 * core, 2)], cot_t.at[pl.ds(1 + 2 * core, 2)],
        c_s.at[0], c_r.at[0], dev(other=True),
    )
    cot_edge = copy(
        cot_t.at[1 + 3 * core], cot_t.at[5 * (1 - core)], c_s.at[1], c_r.at[1], across
    )
    side_copy = copy(planes.at[mine + core], side, c_s.at[2], c_r.at[2], across)
    z_out = []
    for n, d in enumerate(Z_DELTAS):
        z_out.append(put(mine, 2, z_s.at[n], z_r.at[n], dev(dz=d)))
    f_out = [put(mine, 2, f_s.at[0], f_r.at[0], dev(other=True))]

    def edge_copy(i):
        zz = (z + i) % 8
        return copy(
            planes.at[32 - 31 * xl], planes.at[33 * xl],
            b_s.at[i], b_r.at[0], at_space(((1 - xl) * 8 + zz) * 2 + core),
        )

    edge_order = (1, 0, 7, 2, 6, 3, 5, 4)
    z_out[0].start()
    z_out[1].start()
    side_copy.start()
    f_out[0].start()
    cot_core.start()

    @pl.when(edge_sender)
    def _():
        for i in edge_order:
            edge_copy(i).start()

    for c in z_out[2:]:
        c.start()
    cot_edge.start()

    edge_forward = put(edge_slot, 1, bf_s.at[0], bf_r.at[0], dev(other=True))

    def edge_arrive(level):
        @pl.when(jnp.logical_and(edge_receiver, edge_soon == level))
        def _():
            edge_copy(0).wait_recv()
            edge_forward.start()
            build(edge_slot, 1)

        @pl.when(jnp.logical_and(jnp.logical_not(edge_receiver), jnp.maximum(edge_far, 1) == level))
        def _():
            edge_forward.wait_recv()
            build(edge_slot, 1)

    def from_chip(n):
        return 1 + 4 * ((z + 8 - Z_DELTAS[n]) % 8)

    def arrive(n):
        z_out[n].wait_recv()
        c = put(from_chip(n) + 2 * core, 2, f_s.at[n + 1], f_r.at[n + 1], dev(other=True))
        c.start()
        f_out.append(c)

    build(33 * xl, 1)
    build(mine, 2)
    f_out[0].wait_recv()
    build(1 + 4 * z + 2 * (1 - core), 2)
    arrive(0)
    arrive(1)
    beside = 4 * z + 5 * (1 - core)

    @pl.when(jnp.logical_and(beside > 0, beside < 33))
    def _():
        build(beside, 1)

    side_copy.wait_recv()

    @pl.when(jnp.logical_and(s > 0, s < 31))
    def _():
        build_from(side[...].astype(F32), 4 * z + 5 * core)

    edge_arrive(0)

    cot_core.wait_recv()
    cot_cat = jnp.concatenate([cot_t[1], cot_t[2], cot_t[3], cot_t[4]], axis=1)

    def patch_cat(first, offset):
        return jnp.concatenate(
            [
                shifted[pl.ds(aligned((first + i - 1) * ROWS + offset, 64), HALF), :]
                for i in range(4)
            ],
            axis=1,
        )

    w_part = nt(cot_cat, patch_cat(4 * z + 1, core * HALF)).astype(BF16)
    g_part = nt(cot_cat, cot_cat).astype(BF16)
    for r in range(8):
        send_g[0, r] = w_part[r * 16 : r * 16 + 16, :512]
        send_g[1, r, :, :384] = w_part[r * 16 : r * 16 + 16, 512:]
        send_g[1, r, :, 384:] = g_part[r * 16 : r * 16 + 16]
    g_out = []
    for n, (dx, dy) in enumerate(XY_DELTAS):
        x2, y2 = (x + dx) % 4, (y + dy) % 4
        c = copy(
            send_g.at[x2 % 2, (x2 // 2) * 4 + y2], recv_g.at[n],
            g_s.at[n], g_r.at[n], dev(dx, dy),
        )
        c.start()
        g_out.append(c)

    first_row = SHARE * (2 * z + core)
    base = (first_row // 16) * 16
    off = first_row % 16

    def choose(i, carry):
        for t in range(2):
            start = aligned((i - 1) * ROWS + t * 16 * SHARE + base, 16)
            rows_tmp[t] = shifted[pl.ds(start, 80), :].astype(F32)
            chosen[i, t * 64 : t * 64 + 64, :] = rows_tmp[t, pl.ds(off, 64), :].astype(BF16)
        return carry

    chosen[0] = jnp.zeros((128, CELLS), BF16)
    chosen[33] = jnp.zeros((128, CELLS), BF16)

    def covariance(chips, fresh=False):
        for chip in chips:
            for i in range(6):
                choose(jnp.clip(4 * chip + i, 1, 32), 0)
        spots = [4 * chip + 1 + q for chip in chips for q in range(4)]
        left = jnp.concatenate(
            [shifted[pl.ds(aligned(i * ROWS, 64), ROWS), :] for i in spots], axis=1
        )
        right = jnp.concatenate(
            [jnp.concatenate([chosen[i - k] for i in spots], axis=1) for k in (-1, 0, 1)], axis=0
        )
        if fresh:
            acc[...] = nt(left, right)
        else:
            acc[...] += nt(left, right)

    toward = 1 - 2 * core

    def chip_at(d):
        return (z + 8 + d * toward) % 8

    def direct(*news):
        for n in news:
            arrive(n)
        for n in news:
            build(from_chip(n) + 2 * core, 2)

    def forwarded(*news):
        for n in news:
            f_out[n + 1].wait_recv()
        for n in news:
            build(from_chip(n) + 2 * (1 - core), 2)

    arrive(2)
    arrive(3)
    for n in range(4):
        build(from_chip(n) + 2 * core, 2)
    forwarded(0, 1)
    edge_arrive(1)
    covariance((z, chip_at(1)), fresh=True)
    direct(4, 5)
    forwarded(2, 3)
    edge_arrive(2)
    covariance((chip_at(-1), chip_at(2)))
    direct(6)
    forwarded(4, 5)
    total = send_g[xl, j].astype(F32)
    for n in range(15):
        g_out[n].wait_recv()
        total += recv_g[n].astype(F32)
    zsend[...] = total.astype(BF16)
    q_out = []
    for n, d in enumerate(Z_DELTAS):
        c = copy(zsend, zrecv.at[n], q_s.at[n], q_r.at[n], dev(dz=d))
        c.start()
        q_out.append(c)

    edge_arrive(3)
    covariance((chip_at(-2), chip_at(3)))
    forwarded(6)
    covariance((chip_at(-3), chip_at(4)))

    @pl.when(xl == 0)
    def _():
        acc[:, 256:] += nt(shifted[33 * ROWS : 34 * ROWS, :], chosen[32])

    @pl.when(xl == 1)
    def _():
        acc[:, :128] += nt(shifted[:ROWS, :], chosen[1])

    def column_tile(k):
        parts = []
        start, stop = 128 * k, min(128 * k + 128, KC)
        while start < stop:
            kx, row = start // ROWS, start % ROWS
            deep = min(stop - start, ROWS - row)
            parts.append(acc[row : row + deep, kx * 128 : kx * 128 + 128])
            start += deep
        return jnp.transpose(jnp.concatenate(parts, axis=0)).astype(BF16)

    a_out = []
    for n, (dx, dy) in enumerate(XY_DELTAS):
        x2, y2 = (x + dx) % 4, (y + dy) % 4
        a_out.append(
            copy(
                send_a.at[x2 % 2, (x2 // 2) * 4 + y2], recv_a.at[n],
                a_s.at[n], a_r.at[n], dev(dx, dy),
            )
        )
    for h in range(2):
        for k in range(7):
            tile = column_tile(7 * h + k)
            wide = tile.shape[1]
            for t in range(2):
                for q in range(4):
                    send_a[t, 2 * q + h, :, k * 128 : k * 128 + wide] = tile[
                        t * 64 + q * 16 : t * 64 + q * 16 + 16
                    ]
    for c in a_out:
        c.start()

    loads[2].wait()
    for p in range(2):
        patch = shifted[pl.ds(aligned((mine + p - 1) * ROWS, 64), KC), :]
        cells_tmp[p] = tn(patch, weight_t[...])
    for p in range(2):
        for zz in range(NZ):
            out_ref[p, :, zz * 128 : zz * 128 + 128] = cells_tmp[
                p, pl.ds(zz, NY, stride=NZ), :
            ].astype(BF16)

    cot_edge.wait_recv()

    @pl.when(s == 0)
    def _():
        cot_t[0] = jnp.zeros((COUT, CELLS), BF16)

    @pl.when(s == 31)
    def _():
        cot_t[5] = jnp.zeros((COUT, CELLS), BF16)

    w_cat = jnp.concatenate([weight_t[r * ROWS : (r + 1) * ROWS, :] for r in range(3)], axis=1)
    for p in range(2):
        here = 1 + 2 * core + p
        c_cat = jnp.concatenate([cot_t[here + 1], cot_t[here], cot_t[here - 1]], axis=0)
        spread = nn(w_cat, c_cat)
        back = jnp.zeros((CIN, CELLS), F32)
        for n in range(9):
            dy, dz = n // 3 - 1, n % 3 - 1
            part = spread[n * CIN : (n + 1) * CIN]
            turn = (dy * NZ + dz) % CELLS
            if turn:
                part = pltpu.roll(part, turn, 1)
            back += jnp.where(within(-dy, -dz), part, 0.0)
        cells_tmp[2 + p] = jnp.transpose(jnp.concatenate([back, back], axis=0))
    for p in range(2):
        for zp in range(NZ // 2):
            even = cells_tmp[2 + p, pl.ds(2 * zp, NY, stride=NZ), :]
            odd = cells_tmp[2 + p, pl.ds(2 * zp + 1, NY, stride=NZ), :]
            igrad_ref[p, :, zp * 128 : zp * 128 + 128] = jnp.where(lane[:NY] < 64, even, odd).astype(BF16)

    total = zsend[...].astype(F32)
    for n in range(7):
        q_out[n].wait_recv()
        total += zrecv[n].astype(F32)
    quarter = core * 2 + xl
    quarters[quarter] = total.astype(BF16)
    k_out = []
    for n, (device, other) in enumerate(
        ((xl_other, 3 - quarter), (xl_peer, core * 2 + 1 - xl), (dev(other=True), (1 - core) * 2 + xl))
    ):
        c = copy(quarters.at[quarter], quarters.at[quarter], k_s.at[n], k_r.at[n], device)
        c.start()
        k_out.append(c)
    loads[3].wait()
    ainv = ainv_ref[...]
    a_hi = ainv.astype(BF16)
    a_lo = (ainv - a_hi.astype(F32)).astype(BF16)

    piece = send_a[xl, j].astype(F32)
    for n in range(15):
        a_out[n].wait_recv()
        piece += recv_a[n].astype(F32)
    fin[j] = (piece * (1.0 / TOTAL)).astype(BF16)
    v_out = []
    for n, (dx, dy) in enumerate(SAMPLE_DELTAS):
        c = copy(fin.at[j], fin.at[j], v_s.at[n], v_r.at[n], dev(dx, dy))
        c.start()
        v_out.append(c)

    for c in k_out:
        c.wait_recv()
    grad = jnp.concatenate(
        [quarters[0], quarters[1, :, :384], quarters[2], quarters[3, :, :384]], axis=1
    )[:, :KC]
    half = (nt(grad, a_hi) + nt(grad, a_lo)) * (1.0 / TOTAL)
    hg[j, :, :128] = jnp.concatenate([half, jnp.zeros((16, 128 - SHARE), F32)], axis=1).astype(BF16)
    hg[j, :, 128:] = quarters[1, :, 384:]
    u_out = []
    for n, (dx, dy) in enumerate(SAMPLE_DELTAS):
        c = copy(hg.at[j], hg.at[j], u_s.at[n], u_r.at[n], dev(dx, dy))
        c.start()
        u_out.append(c)

    for c in v_out:
        c.wait_recv()
    for c in u_out:
        c.wait_recv()

    for c in z_out + f_out + [cot_core, cot_edge, side_copy] + g_out + q_out + k_out + a_out + v_out + u_out:
        c.wait_send()

    @pl.when(edge_receiver)
    def _():
        edge_forward.wait_send()

    @pl.when(edge_sender)
    def _():
        for i in range(8):
            edge_copy(i).wait_send()


def finish_kernel(
    fin_ref, out_in, igrad_in, hg_ref, ginv_ref, out_ref, igrad_ref, a_ref, g_ref, update_ref
):
    out_ref[...] = out_in[...]
    igrad_ref[...] = igrad_in[...]
    for q in range(4):
        deep = min(16, SHARE - 16 * q)
        a_ref[16 * q : 16 * q + deep, :HALF] = fin_ref[2 * q][:deep].astype(F32)
        a_ref[16 * q : 16 * q + deep, HALF:] = fin_ref[2 * q + 1][:deep, : KC - HALF].astype(F32)
    hg = hg_ref[...].reshape(COUT, 256)
    g_ref[...] = hg[:, 128:].astype(F32) * (1.0 / TOTAL)
    update = lax.dot_general(
        ginv_ref[...], hg[:, :128].astype(F32), (((1,), (0,)), ((), ())),
        precision=lax.Precision.HIGHEST, preferred_element_type=F32,
    )
    update_ref[...] = jnp.transpose(update)[:SHARE]


def shards(activations, cotangent, weight, a_inverse, g_inverse):
    vmem = pl.BlockSpec(memory_space=pltpu.VMEM)
    dma = pltpu.SemaphoreType.DMA
    counts = (7, 7, 8, 8, 8, 1, 1, 1, 3, 3, 15, 15, 7, 7, 3, 3, 7, 7, 15, 15, 7, 7)
    fin, outs, igrad, hg = pl.pallas_call(
        step_kernel,
        out_shape=(
            pltpu.VMEM((8, 16, HALF), BF16),
            pltpu.VMEM((2, NY, NZ * COUT), BF16),
            pltpu.VMEM((2, NY, NZ * CIN), BF16),
            pltpu.VMEM((8, 16, 256), BF16),
        ),
        in_specs=[pl.BlockSpec(memory_space=pltpu.HBM)] * 4,
        out_specs=[vmem] * 4,
        scratch_shapes=[
            pltpu.VMEM((PLANES, CIN, CELLS), BF16),
            pltpu.VMEM(((PLANES + 1) * ROWS, CELLS), BF16),
            pltpu.VMEM((34, 128, CELLS), BF16),
            pltpu.VMEM((ROWS, 384), F32),
            pltpu.VMEM((CIN, CELLS), BF16),
            pltpu.VMEM((2, 80, CELLS), F32),
            pltpu.VMEM((4, CELLS, 128), F32),
            pltpu.VMEM((6, COUT, CELLS), BF16),
            pltpu.VMEM((2, NY, NZ * CIN), BF16),
            pltpu.VMEM((2, NY, NZ * COUT), BF16),
            pltpu.VMEM((KC, COUT), BF16),
            pltpu.VMEM((SHARE, KC), F32),
            dma((4,)),
            pltpu.VMEM((2, 8, 16, HALF), BF16),
            pltpu.VMEM((15, 16, HALF), BF16),
            pltpu.VMEM((2, 8, 16, 512), BF16),
            pltpu.VMEM((15, 16, 512), BF16),
            pltpu.VMEM((16, 512), BF16),
            pltpu.VMEM((7, 16, 512), BF16),
            pltpu.VMEM((4, 16, 512), BF16),
        ]
        + [dma((n,)) for n in counts],
        compiler_params=pltpu.CompilerParams(
            collective_id=0, has_side_effects=True, vmem_limit_bytes=58 << 20
        ),
        cost_estimate=pl.CostEstimate(flops=2 * 10**9, bytes_accessed=2 * 10**6, transcendentals=0),
        name="step",
    )(activations[0], cotangent[0], weight.T, a_inverse)
    outputs, input_grad, a_factor, g_factor, update = pl.pallas_call(
        finish_kernel,
        out_shape=(
            jax.ShapeDtypeStruct((2, NY, NZ * COUT), BF16),
            jax.ShapeDtypeStruct((2, NY, NZ * CIN), BF16),
            jax.ShapeDtypeStruct((SHARE, KC), F32),
            jax.ShapeDtypeStruct((COUT, COUT), F32),
            jax.ShapeDtypeStruct((SHARE, COUT), F32),
        ),
        in_specs=[vmem] * 5,
        out_specs=[vmem] * 5,
        compiler_params=pltpu.CompilerParams(vmem_limit_bytes=16 << 20),
        name="finish",
    )(fin, outs, igrad, hg, g_inverse)
    return outputs[None], input_grad[None], a_factor, g_factor, update.T


def solution(mesh):
    return jax.shard_map(
        shards,
        mesh=mesh,
        in_specs=(
            P("sample", "space", None, None),
            P("sample", "space", None, None),
            P(),
            P("space", None),
            P(),
        ),
        out_specs=(
            P("sample", "space", None, None),
            P("sample", "space", None, None),
            P("space", None),
            P(),
            P(None, "space"),
        ),
        check_vma=False,
    )
```
